512 devices in a mesh: dp: 32 (over x, y_hi, core), expert: 16 (over y_lo, z).
Axes of the slice: x: 4, y: 8 (y_hi: 4, y_lo: 2; y = y_hi * 2 + y_lo), z: 8, core: 2. Of those that a mesh axis runs over, the one named last changes fastest.
Arguments:
- tokens: bfloat16 [1024, 8192], P('expert', 'dp'), may hold values from -6 to 6
- gate_up: bfloat16 [16, 8192, 3584], P('expert', 'dp'), may hold values from -0.0625 to 0.0625
- down: bfloat16 [16, 1792, 8192], P('expert', None, 'dp'), may hold values from -0.125 to 0.125
- expert_ids: int32 [1024, 2], P('expert'), may hold values from 0 to 15, all different within a row; in each aligned block of 64 rows (0 to 63, 64 to 127, ...) at most 12 rows name the same one
- gate_values: float32 [1024, 2], P('expert'), may hold values from 0.1 to 0.6
- out_grad: bfloat16 [1024, 8192], P('expert', 'dp'), may hold values from -1.5 to 1.5
Outputs:
- moe_out: bfloat16 [1024, 8192], P('expert', 'dp')
- token_grad: bfloat16 [1024, 8192], P('expert', 'dp')
The draws below stay inside these ranges and needn't reach their ends.
Inputs may be any that keep to these rules, and one draw needn't show every extreme that they name: `expert_ids`: each row names 2 different experts. Among the 64 rows of one device no expert is named more than 12 times, and in some device's rows one expert is named exactly 12 times.
All inputs are finite; a program needn't handle non-finite values.
Results may differ from the reference program's by a relative error of at most 0.0065.
Values may be sent and summed in bfloat16 or wider, within the bound.
No kernel may reach another device: no remote copies, remote signals or barrier semaphores. Data moves between devices by JAX's collectives and lax.ppermute only.
A program may use at most 64 MiB of HBM per device.

```python
import math
import jax
import jax.numpy as jnp
import numpy as np
from jax import lax

D = 8192
F = 1792
TOPK = 2
TOK_DEV = 64
EXPERTS = 16
CAP = 12
ROWS = 192
TOKENS = 1024
N_EXPERT = 16


def levels(own_key, dims, shards, smallest, largest):
    def one(dim, blocks):
        heights = jax.random.uniform(jax.random.fold_in(jax.random.fold_in(own_key, 6), dim), (blocks,), jnp.float32, smallest / len(shards), largest / len(shards))
        return jnp.repeat(jnp.exp(heights), dims[dim] // blocks).reshape((-1,) + (1,) * (len(dims) - dim - 1))

    loudness = one(*shards[0])
    for cut in shards[1:]:
        loudness = loudness * one(*cut)
    return loudness


def shared_out(key, own, number, rows, number_of, top, bound, skew):
    sequence = jax.random.permutation(key, number_of)
    heavy_load, ordinary = shares(number_of, rows * top, bound, skew, True), shares(number_of, rows * top, bound, skew, False)
    places = jnp.arange(number_of)

    def named(sizes, turn):
        used = int((sizes > 0).sum())
        fixed = max(1, used // 4)
        moved = fixed + (places - fixed + turn * (used - fixed)) % max(1, number_of - fixed)
        return jnp.zeros((number_of,), jnp.int32).at[sequence[jnp.where(places < fixed, places, moved)]].set(jnp.asarray(sizes, jnp.int32))

    sizes = jnp.where(number % 4 == 0, named(heavy_load, number // 4), named(ordinary, number - number // 4 - 1))
    mixed = jax.random.permutation(jax.random.fold_in(own, 3), number_of)
    donor, receiver = mixed[0:number_of // 2 * 2:2], mixed[1:number_of // 2 * 2:2]
    slack = jnp.minimum(sizes[donor] - 1, bound - sizes[receiver]) // 2
    slack = jnp.where((donor == sequence[0]) | (receiver == sequence[0]) | (sizes[receiver] == 0), 0, jnp.maximum(slack, 0))
    moved = jax.random.randint(jax.random.fold_in(own, 4), (number_of // 2,), 0, 1 << 20) % (slack + 1)
    sizes = sizes.at[donor].add(-moved).at[receiver].add(moved)
    labels = jnp.searchsorted(jnp.cumsum(sizes), jnp.arange(rows * top), side="right").astype(jnp.int32)
    listing = labels.reshape(top, rows).T
    listing = listing[jax.random.permutation(jax.random.fold_in(own, 1), rows)]
    turn = jax.random.randint(jax.random.fold_in(own, 2), (rows, 1), 0, top)
    return jnp.take_along_axis(listing, (jnp.arange(top)[None, :] + turn) % top, axis=1)


def shares(count, total, bound, slope, full):
    portions = [(1 << 20) // math.isqrt(grade ** slope) + 1 for grade in range(1, count + 1)]
    largest = bound if full else min(bound, max(-(-total // count), total * portions[0] // sum(portions)))
    least = 1 if total - largest >= count - 1 else 0
    given, spare = [largest] + [least] * (count - 1), total - largest - least * (count - 1)
    while spare > 0:
        movable = [i for i in range(1, count) if given[i] < largest] or [i for i in range(1, count) if given[i] < bound]
        pool, budget = sum([portions[i] for i in movable]), spare
        for i in movable:
            addition = min(bound - given[i], max(1, budget * portions[i] // pool), spare)
            given[i] = given[i] + addition
            spare = spare - addition
    return np.array(given)


def bell_draw(stream_key, extent, scale, limit, split=(), held_as=jnp.bfloat16):
    entries = scale * jax.random.normal(stream_key, extent, jnp.float32)
    if split:
        entries = entries * levels(stream_key, extent, split, -0.22, 0.18)
    return jnp.clip(entries, -limit, limit).astype(held_as)


def setup_inputs(seed: int = 0) -> dict:
    seeds = jax.random.split(jax.random.key(seed), 7)
    tokens = bell_draw(seeds[0], (TOKENS, D), 1.0, 6.0, ((0, 16), (1, 32)))
    gate_up = bell_draw(seeds[1], (EXPERTS, D, 2 * F), D ** -0.5, 0.0625, ((0, 16), (1, 32)))
    down = bell_draw(seeds[2], (EXPERTS, F, D), F ** -0.5, 0.125, ((0, 16), (2, 32)))
    expert_ids_keys = jax.random.split(jax.random.fold_in(seeds[3], 1), TOKENS // TOK_DEV)
    expert_ids_turns = jax.random.permutation(jax.random.fold_in(seeds[3], 3), TOKENS // TOK_DEV)
    expert_ids = jax.vmap(lambda own, number: shared_out(jax.random.fold_in(seeds[3], 2), own, number, TOK_DEV, EXPERTS, TOPK, CAP, 2))(expert_ids_keys, expert_ids_turns).reshape((TOKENS, TOPK))
    gate_values = jnp.clip(0.1 + 0.5 * jax.random.uniform(seeds[4], (TOKENS, TOPK), jnp.float32) ** levels(seeds[4], (TOKENS, TOPK), ((0, 16),), -0.2, 0.2), 0.1, 0.6)
    out_grad = bell_draw(seeds[5], (TOKENS, D), 0.25, 1.5, ((0, 16), (1, 32)))
    return {"tokens": tokens, "gate_up": gate_up, "down": down, "expert_ids": expert_ids, "gate_values": gate_values, "out_grad": out_grad}


def positions(expert_ids):
    blocks = expert_ids.reshape(N_EXPERT, TOK_DEV * TOPK)
    onehot = (blocks[:, :, None] == jnp.arange(EXPERTS, dtype=jnp.int32)).astype(jnp.int32)
    slot_rank = jnp.sum((jnp.cumsum(onehot, axis=1) - 1) * onehot, axis=2)
    anchor = jnp.arange(N_EXPERT, dtype=jnp.int32)[:, None] * CAP
    return (anchor + slot_rank).reshape(TOKENS, TOPK).astype(jnp.int32)


def to_experts(values, expert_ids, slot_rows):
    buffer = jnp.zeros((EXPERTS, ROWS, D), values.dtype)
    return buffer.at[expert_ids.reshape(-1), slot_rows.reshape(-1)].set(values.reshape(TOKENS * TOPK, D))


def expert_pass(operands):
    token_slots, grad_slots, gate_up, down = operands
    projected = jnp.dot(token_slots, gate_up, preferred_element_type=jnp.float32)
    gate_pre = projected[:, :F]
    up_pre = projected[:, F:]
    sigmoid_gate = jax.nn.sigmoid(gate_pre)
    hidden = (gate_pre * sigmoid_gate * up_pre).astype(jnp.bfloat16)
    outputs = jnp.dot(hidden, down, preferred_element_type=jnp.float32).astype(jnp.bfloat16)
    hidden_grad = jnp.dot(grad_slots, down.T, preferred_element_type=jnp.float32)
    gate_grad = hidden_grad * up_pre * sigmoid_gate * (1.0 + gate_pre * (1.0 - sigmoid_gate))
    up_grad = hidden_grad * gate_pre * sigmoid_gate
    pre_grad = jnp.concatenate([gate_grad, up_grad], axis=1).astype(jnp.bfloat16)
    input_grad = jnp.dot(pre_grad, gate_up.T, preferred_element_type=jnp.float32).astype(jnp.bfloat16)
    return outputs, input_grad


def reference(tokens, gate_up, down, expert_ids, gate_values, out_grad):
    slot_rows = positions(expert_ids)
    token_copies = jnp.broadcast_to(tokens[:, None, :], (TOKENS, TOPK, D))
    scaled = (gate_values[:, :, None] * out_grad[:, None, :].astype(jnp.float32)).astype(jnp.bfloat16)
    token_slots = to_experts(token_copies, expert_ids, slot_rows)
    grad_slots = to_experts(scaled, expert_ids, slot_rows)
    outputs, input_grad = lax.map(expert_pass, (token_slots, grad_slots, gate_up, down))
    picked = outputs[expert_ids, slot_rows].astype(jnp.float32)
    moe_out = jnp.sum(gate_values[:, :, None] * picked, axis=1).astype(jnp.bfloat16)
    token_grad = jnp.sum(input_grad[expert_ids, slot_rows].astype(jnp.float32), axis=1).astype(jnp.bfloat16)
    return moe_out, token_grad
```

```python
import functools

import jax
import jax.numpy as jnp
from jax import lax
from jax.experimental import pallas as pl
from jax.experimental.pallas import tpu as pltpu
from jax.sharding import Mesh, PartitionSpec as P

BF16 = jnp.bfloat16
F32 = jnp.float32
NX, NY, NC, NL, NZ = 4, 4, 2, 2, 8
TOK, TOPK, E, CAP = 64, 2, 16, 12
PAIR = 2 * CAP
ROWS = E * CAP
SEND = E * PAIR
DW = 256
F = 1792
H = F // NC
RX = ROWS // NX
VMEM = pl.BlockSpec(memory_space=pltpu.VMEM)


def mm(a, b):
    return lax.dot_general(a, b, (((1,), (0,)), ((), ())), preferred_element_type=F32)


def mm_t(a, b):
    return lax.dot_general(a, b, (((1,), (1,)), ((), ())), preferred_element_type=F32)


def iota(shape, dim):
    return lax.broadcasted_iota(jnp.int32, shape, dim)


def onehot(cond):
    return jnp.where(cond, 1.0, 0.0).astype(BF16)


def call(kernel, out_shape, count, limit_mb=12):
    return pl.pallas_call(
        kernel,
        out_shape=out_shape,
        in_specs=[VMEM] * count,
        out_specs=jax.tree.map(lambda _: VMEM, out_shape),
        compiler_params=pltpu.CompilerParams(vmem_limit_bytes=limit_mb << 20),
    )


def pack_kernel(ids_ref, gate_ref, tok_ref, grad_ref, send_ref, place_ref):
    ids = ids_ref[...]
    hots = [(ids[:, k : k + 1] == iota((TOK, E), 1)).astype(F32) for k in range(TOPK)]
    lower = onehot(iota((TOK, TOK), 1) < iota((TOK, TOK), 0))
    earlier = mm(lower, (hots[0] + hots[1]).astype(BF16))
    eye = iota((TOK, TOK), 0) == iota((TOK, TOK), 1)
    row = iota((SEND, TOK), 0)
    grad = grad_ref[...].astype(F32)
    pick_tok = jnp.zeros((SEND, TOK), BF16)
    total = jnp.zeros((SEND, DW), F32)
    places = []
    for k in range(TOPK):
        rank = jnp.sum(hots[k] * earlier, axis=1, keepdims=True).astype(jnp.int32)
        place = ids[:, k : k + 1] * PAIR + rank
        places.append(place)
        across = jnp.sum(jnp.where(eye, place, 0), axis=0, keepdims=True)
        pick_tok += onehot(row == across)
        scaled = (gate_ref[:, k : k + 1] * grad).astype(BF16)
        total += mm(onehot(row == across + CAP), scaled)
    total += mm(pick_tok, tok_ref[...])
    send_ref[...] = total.astype(BF16)
    place_ref[...] = jnp.concatenate(places, axis=1)


def slot_to_pair(slot):
    extra = jnp.zeros_like(slot)
    for b in range(1, E):
        extra += jnp.where(slot >= b * CAP, CAP, 0)
    return slot + extra


def half_columns(c):
    return pl.ds(pl.multiple_of(c * H, H), H), pl.ds(pl.multiple_of(F + c * H, H), H)


def partials(x, g, wgu_ref, wd_ref, c):
    gate, up = half_columns(c)
    return mm(x, wgu_ref[:, gate]), mm(x, wgu_ref[:, up]), mm_t(g, wd_ref[gate, :])


def away_kernel(arr_ref, wgu_ref, wd_ref, out_ref, x_ref, g_ref):
    arrived = arr_ref[...]
    source = slot_to_pair(iota((ROWS, 1), 0))
    col = iota((ROWS, SEND), 1)
    x_ref[...] = mm(onehot(col == source), arrived).astype(BF16)
    g_ref[...] = mm(onehot(col == source + CAP), arrived).astype(BF16)
    terms = partials(x_ref[...], g_ref[...], wgu_ref, wd_ref, 1 - lax.axis_index("c"))
    for j, term in enumerate(terms):
        out_ref[:, j * H : (j + 1) * H] = term.astype(BF16)


def home_kernel(x_ref, g_ref, wgu_ref, wd_ref, got_ref, out_ref, own_ref):
    c, i = lax.axis_index("c"), lax.axis_index("x")
    terms = partials(x_ref[...], g_ref[...], wgu_ref, wd_ref, c)
    for j, term in enumerate(terms):
        cols = slice(j * H, (j + 1) * H)
        out_ref[:, cols] = (term + got_ref[:, cols].astype(F32)).astype(BF16)
    rows = pl.ds(pl.multiple_of(i * RX, RX), RX)
    terms = partials(x_ref[rows, :], g_ref[rows, :], wgu_ref, wd_ref, c)
    for j, term in enumerate(terms):
        cols = slice(j * H, (j + 1) * H)
        own_ref[:, cols] = term + got_ref[rows, cols].astype(F32)


def sum_x_kernel(got_ref, own_ref, out_ref, rest_ref):
    i = lax.axis_index("x")
    total = own_ref[...] - got_ref[i].astype(F32)
    for j in range(NX):
        total += got_ref[j].astype(F32)
    rounded = total.astype(BF16)
    out_ref[...] = rounded
    rest_ref[...] = total - rounded.astype(F32)


def act_kernel(part_ref, rest_ref, out_ref):
    total = rest_ref[...]
    for i in range(NY):
        total += part_ref[i].astype(F32)
    gate, up, hg = total[:, :H], total[:, H : 2 * H], total[:, 2 * H :]
    sig = jax.nn.sigmoid(gate)
    silu = gate * sig
    out_ref[:, :H] = (silu * up).astype(BF16)
    out_ref[:, H : 2 * H] = (hg * up * sig * (1.0 + gate * (1.0 - sig))).astype(BF16)
    out_ref[:, 2 * H :] = (hg * silu).astype(BF16)


def finish_kernel(act_ref, wgu_ref, wd_ref, send_ref):
    act = act_ref[...].reshape(NX, NC, RX, 3 * H)
    out = jnp.zeros((ROWS, DW), F32)
    back = jnp.zeros((ROWS, DW), F32)
    for c in range(NC):
        a = act[:, c].reshape(ROWS, 3 * H)
        out += mm(a[:, :H], wd_ref[c * H : (c + 1) * H, :])
        back += mm_t(a[:, H : 2 * H], wgu_ref[:, c * H : (c + 1) * H])
        back += mm_t(a[:, 2 * H :], wgu_ref[:, F + c * H : F + (c + 1) * H])
    row = iota((SEND, ROWS), 0)
    target = jnp.where(iota((1, ROWS), 1) >= 0, slot_to_pair(iota((1, ROWS), 1)), 0)
    send = mm(onehot(row == target), out.astype(BF16))
    send += mm(onehot(row == target + CAP), back.astype(BF16))
    send_ref[...] = send.astype(BF16)


def combine_kernel(ret_ref, gate_ref, place_ref, moe_ref, tok_ref):
    returned = ret_ref[...]
    col = iota((TOK, SEND), 1)
    place = place_ref[...]
    moe = jnp.zeros((TOK, DW), F32)
    pick = jnp.zeros((TOK, SEND), BF16)
    for k in range(TOPK):
        at = place[:, k : k + 1]
        moe += gate_ref[:, k : k + 1] * mm(onehot(col == at), returned)
        pick += onehot(col == at + CAP)
    moe_ref[...] = moe.astype(BF16)
    tok_ref[...] = mm(pick, returned).astype(BF16)


def local(tokens, gate_up, down, expert_ids, gate_values, out_grad):
    wgu, wd = gate_up[0], down[0]
    send, place = call(
        pack_kernel,
        (jax.ShapeDtypeStruct((SEND, DW), BF16), jax.ShapeDtypeStruct((TOK, TOPK), jnp.int32)),
        4,
    )(expert_ids, gate_values, tokens, out_grad)
    arrived = lax.all_to_all(
        send.reshape(E, PAIR, DW), ("yl", "z"), 0, 0, tiled=True
    ).reshape(SEND, DW)
    wide, narrow = jax.ShapeDtypeStruct((ROWS, 3 * H), BF16), jax.ShapeDtypeStruct((ROWS, DW), BF16)
    chunk16, chunk32 = (jax.ShapeDtypeStruct((RX, 3 * H), t) for t in (BF16, F32))
    away, x, g = call(away_kernel, (wide, narrow, narrow), 3)(arrived, wgu, wd)
    got = lax.ppermute(away, "c", [(0, 1), (1, 0)])
    chip, own = call(home_kernel, (wide, chunk32), 5)(x, g, wgu, wd, got)
    got = lax.all_to_all(chip.reshape(NX, RX, 3 * H), "x", 0, 0, tiled=True)
    chunk, rest = call(sum_x_kernel, (chunk16, chunk32), 2)(got, own)
    parts = lax.all_gather(chunk, "yh", axis=0)
    act = call(act_kernel, chunk16, 2)(parts, rest)
    acts = lax.all_gather(act, ("x", "c"), axis=0)
    back = call(finish_kernel, jax.ShapeDtypeStruct((SEND, DW), BF16), 3)(acts, wgu, wd)
    returned = lax.all_to_all(
        back.reshape(E, PAIR, DW), ("yl", "z"), 0, 0, tiled=True
    ).reshape(SEND, DW)
    shape = jax.ShapeDtypeStruct((TOK, DW), BF16)
    return call(combine_kernel, (shape, shape), 3)(returned, gate_values, place)


def solution(mesh):
    fine = Mesh(mesh.devices.reshape(NX, NY, NC, NL, NZ), ("x", "yh", "c", "yl", "z"))
    dp, ex = ("x", "yh", "c"), ("yl", "z")
    return jax.shard_map(
        local,
        mesh=fine,
        in_specs=(
            P(ex, dp),
            P(ex, dp, None),
            P(ex, None, dp),
            P(ex, None),
            P(ex, None),
            P(ex, dp),
        ),
        out_specs=(P(ex, dp), P(ex, dp)),
        check_vma=False,
    )
```

```python
import jax
import jax.numpy as jnp
from jax import lax
from jax.experimental import pallas as pl
from jax.experimental.pallas import tpu as pltpu
from jax.sharding import PartitionSpec as P

BF16 = jnp.bfloat16
F32 = jnp.float32
NX, NY, NC = 4, 4, 2
RING = 4

TOK, TOPK, E, CAP = 64, 2, 16, 12
PAIR = 2 * CAP
ROWS = E * CAP
SEND = E * PAIR
DW = 256
F = 1792
H = F // NC
RX = ROWS // RING

ALONG_X = [[[(x * NY + y) * NC + c for x in range(NX)] for y in range(NY)] for c in range(NC)]
ALONG_Y = [[[(x * NY + y) * NC + c for y in range(NY)] for x in range(NX)] for c in range(NC)]
FIRST = ALONG_X[0] + ALONG_Y[1]
SECOND = ALONG_Y[0] + ALONG_X[1]
SWAP = [(i, i ^ 1) for i in range(NX * NY * NC)]
VMEM = pl.BlockSpec(memory_space=pltpu.VMEM)


def core():
    return lax.rem(lax.axis_index("dp"), NC)


def place_in_first():
    d = lax.axis_index("dp")
    x, y = lax.div(d, NY * NC), lax.rem(lax.div(d, NC), NY)
    return jnp.where(core() == 0, x, y)


def mm(a, b):
    return lax.dot_general(a, b, (((1,), (0,)), ((), ())), preferred_element_type=F32)


def mm_t(a, b):
    return lax.dot_general(a, b, (((1,), (1,)), ((), ())), preferred_element_type=F32)


def iota(shape, dim):
    return lax.broadcasted_iota(jnp.int32, shape, dim)


def onehot(cond):
    return jnp.where(cond, 1.0, 0.0).astype(BF16)


def call(kernel, out_shape, count, limit_mb=12, flops=0, nbytes=0, **kw):
    kw.setdefault("in_specs", [VMEM] * count)
    return pl.pallas_call(
        kernel,
        out_shape=out_shape,
        out_specs=jax.tree.map(lambda _: VMEM, out_shape),
        compiler_params=pltpu.CompilerParams(vmem_limit_bytes=limit_mb << 20),
        cost_estimate=pl.CostEstimate(flops=flops, bytes_accessed=nbytes, transcendentals=0),
        **kw,
    )


def turned(row, eye):
    return jnp.sum(jnp.where(eye, row, jnp.zeros_like(row)), axis=1, keepdims=True)


def pack_kernel(
    ids_hbm, gate_hbm, tok_hbm, grad_hbm, wgu_hbm, wd_hbm,
    send_ref, place_ref, weight_ref, wgu_out, wd_out,
    ids_ref, gate_ref, tok_ref, grad_ref, sems,
):
    pairs = [(ids_hbm, ids_ref), (gate_hbm, gate_ref), (tok_hbm, tok_ref), (grad_hbm, grad_ref)]
    pairs += [(wgu_hbm, wgu_out), (wd_hbm, wd_out)]
    moves = [pltpu.make_async_copy(*pair, sems.at[n]) for n, pair in enumerate(pairs)]
    for move in moves:
        move.start()
    eye = iota((TOK, TOK), 0) == iota((TOK, TOK), 1)
    before = onehot(iota((TOK, TOK), 0) < iota((TOK, TOK), 1))
    row = iota((SEND, TOK), 0)
    moves[0].wait()
    moves[1].wait()
    ids = ids_ref[...]
    hots = [(ids[k : k + 1, :] == iota((E, TOK), 0)).astype(F32) for k in range(TOPK)]
    earlier = mm((hots[0] + hots[1]).astype(BF16), before)
    across, places, weights = [], [], []
    for k in range(TOPK):
        rank = jnp.sum(hots[k] * earlier, axis=0, keepdims=True).astype(jnp.int32)
        place = ids[k : k + 1, :] * PAIR + rank
        across.append(place)
        places.append(turned(place, eye))
        weights.append(turned(gate_ref[k : k + 1, :], eye))
    place_ref[...] = jnp.concatenate(places, axis=1)
    weight_ref[...] = jnp.concatenate(weights, axis=1)
    moves[2].wait()
    pick_tok = onehot((row == across[0]) | (row == across[1]))
    total = mm(pick_tok, tok_ref[...])
    moves[3].wait()
    grad = grad_ref[...].astype(F32)
    for k in range(TOPK):
        total += mm(onehot(row == across[k] + CAP), (weights[k] * grad).astype(BF16))
    send_ref[...] = total.astype(BF16)
    for move in moves[4:]:
        move.wait()


def slot_to_pair(slot):
    extra = jnp.zeros_like(slot)
    for b in range(1, E):
        extra += jnp.where(slot >= b * CAP, CAP, 0)
    return slot + extra


def half_columns(c):
    return pl.ds(pl.multiple_of(c * H, H), H), pl.ds(pl.multiple_of(F + c * H, H), H)


def partials(x, g, wgu_ref, wd_ref, c):
    gate, up = half_columns(c)
    return mm(x, wgu_ref[:, gate]), mm(x, wgu_ref[:, up]), mm_t(g, wd_ref[gate, :])


def away_kernel(arr_ref, wgu_ref, wd_ref, out_ref, x_ref, g_ref):
    arrived = arr_ref[...]
    source = slot_to_pair(iota((ROWS, 1), 0))
    col = iota((ROWS, SEND), 1)
    x_ref[...] = mm(onehot(col == source), arrived).astype(BF16)
    g_ref[...] = mm(onehot(col == source + CAP), arrived).astype(BF16)
    terms = partials(x_ref[...], g_ref[...], wgu_ref, wd_ref, 1 - core())
    for j, term in enumerate(terms):
        out_ref[:, j * H : (j + 1) * H] = term.astype(BF16)


def home_kernel(x_ref, g_ref, wgu_ref, wd_ref, out_ref):
    terms = partials(x_ref[...], g_ref[...], wgu_ref, wd_ref, core())
    for j, term in enumerate(terms):
        out_ref[:, j * H : (j + 1) * H] = term


def add_kernel(home_ref, got_ref, out_ref, own_ref):
    out_ref[...] = (home_ref[...] + got_ref[...].astype(F32)).astype(BF16)
    rows = pl.ds(pl.multiple_of(place_in_first() * RX, RX), RX)
    own_ref[...] = home_ref[rows, :] + got_ref[rows, :].astype(F32)


def sum_kernel(got_ref, own_ref, out_ref, rest_ref):
    i = place_in_first()
    total = own_ref[...] - got_ref[i].astype(F32)
    for j in range(RING):
        total += got_ref[j].astype(F32)
    rounded = total.astype(BF16)
    out_ref[...] = rounded
    rest_ref[...] = total - rounded.astype(F32)


def act_kernel(part_ref, rest_ref, out_ref):
    total = rest_ref[...]
    for i in range(RING):
        total += part_ref[i].astype(F32)
    gate, up, hg = total[:, :H], total[:, H : 2 * H], total[:, 2 * H :]
    sig = jax.nn.sigmoid(gate)
    silu = gate * sig
    out_ref[:, :H] = (silu * up).astype(BF16)
    out_ref[:, H : 2 * H] = (hg * up * sig * (1.0 + gate * (1.0 - sig))).astype(BF16)
    out_ref[:, 2 * H :] = (hg * silu).astype(BF16)


def products(act_ref, wgu_ref, wd_ref, c):
    gate, up = half_columns(c)
    out = mm(act_ref[:, :H], wd_ref[gate, :])
    back = mm_t(act_ref[:, H : 2 * H], wgu_ref[:, gate])
    return out, back + mm_t(act_ref[:, 2 * H :], wgu_ref[:, up])


def first_kernel(act_ref, wgu_ref, wd_ref, out_ref, back_ref):
    out_ref[...], back_ref[...] = products(act_ref, wgu_ref, wd_ref, core())


def finish_kernel(act_ref, wgu_ref, wd_ref, out_ref, back_ref, send_ref):
    out, back = products(act_ref, wgu_ref, wd_ref, 1 - core())
    row = iota((SEND, ROWS), 0)
    target = slot_to_pair(iota((1, ROWS), 1))
    send = mm(onehot(row == target), (out_ref[...] + out).astype(BF16))
    send += mm(onehot(row == target + CAP), (back_ref[...] + back).astype(BF16))
    send_ref[...] = send.astype(BF16)


def combine_kernel(ret_ref, weight_ref, place_ref, moe_ref, tok_ref):
    returned = ret_ref[...]
    col = iota((TOK, SEND), 1)
    place = place_ref[...]
    moe = jnp.zeros((TOK, DW), F32)
    pick = jnp.zeros((TOK, SEND), BF16)
    for k in range(TOPK):
        at = place[:, k : k + 1]
        moe += weight_ref[:, k : k + 1] * mm(onehot(col == at), returned)
        pick += onehot(col == at + CAP)
    moe_ref[...] = moe.astype(BF16)
    tok_ref[...] = mm(pick, returned).astype(BF16)


def local(tokens, gate_up, down, expert_ids, gate_values, out_grad):
    sds = jax.ShapeDtypeStruct
    wide16, wide32 = (sds((ROWS, 3 * H), t) for t in (BF16, F32))
    narrow16, narrow32 = (sds((ROWS, DW), t) for t in (BF16, F32))
    chunk16, chunk32 = (sds((RX, 3 * H), t) for t in (BF16, F32))
    small = [pltpu.VMEM((TOPK, TOK), jnp.int32), pltpu.VMEM((TOPK, TOK), F32)]
    small += [pltpu.VMEM((TOK, DW), BF16)] * 2
    work = dict(flops=2 * ROWS * DW * 3 * H, nbytes=4 << 20)

    send, place, weight, wgu, wd = call(
        pack_kernel,
        (
            sds((SEND, DW), BF16),
            sds((TOK, TOPK), jnp.int32),
            sds((TOK, TOPK), F32),
            sds(gate_up.shape[1:], BF16),
            sds(down.shape[1:], BF16),
        ),
        6,
        in_specs=[pl.BlockSpec(memory_space=pltpu.HBM)] * 6,
        scratch_shapes=small + [pltpu.SemaphoreType.DMA((6,))],
    )(
        *(
            pltpu.with_memory_space_constraint(v, pltpu.HBM)
            for v in (expert_ids.T, gate_values.T, tokens, out_grad, gate_up[0], down[0])
        )
    )
    arrived = lax.all_to_all(
        send.reshape(E, PAIR, DW), "expert", 0, 0, tiled=True
    ).reshape(SEND, DW)
    away, x, g = call(away_kernel, (wide16, narrow16, narrow16), 3, **work)(arrived, wgu, wd)
    got = lax.ppermute(away, "dp", SWAP)
    home = call(home_kernel, wide32, 4, **work)(x, g, wgu, wd)
    chip, own = call(add_kernel, (wide16, chunk32), 2)(home, got)
    got = lax.all_to_all(
        chip.reshape(RING, RX, 3 * H), "dp", 0, 0, axis_index_groups=FIRST, tiled=True
    )
    chunk, rest = call(sum_kernel, (chunk16, chunk32), 2)(got, own)
    parts = lax.all_gather(chunk, "dp", axis=0, axis_index_groups=SECOND)
    act = call(act_kernel, chunk16, 2)(parts, rest)
    mine = lax.all_gather(act, "dp", axis=0, axis_index_groups=FIRST, tiled=True)
    other = lax.ppermute(mine, "dp", SWAP)
    out, back = call(first_kernel, (narrow32, narrow32), 3, **work)(mine, wgu, wd)
    back = call(finish_kernel, sds((SEND, DW), BF16), 5)(other, wgu, wd, out, back)
    returned = lax.all_to_all(
        back.reshape(E, PAIR, DW), "expert", 0, 0, tiled=True
    ).reshape(SEND, DW)
    shape = sds((TOK, DW), BF16)
    return call(combine_kernel, (shape, shape), 3)(returned, weight, place)


def solution(mesh):
    rows, cols = P("expert", "dp"), P("expert", None)
    return jax.shard_map(
        local,
        mesh=mesh,
        in_specs=(rows, P("expert", "dp", None), P("expert", None, "dp"), cols, cols, rows),
        out_specs=(rows, rows),
        check_vma=False,
    )
```

```python
import jax
import jax.numpy as jnp
from jax import lax
from jax.experimental import pallas as pl
from jax.experimental.pallas import tpu as pltpu
from jax.sharding import PartitionSpec as P

BF16 = jnp.bfloat16
F32 = jnp.float32
NX, NY, NC = 4, 4, 2
RING = 4

TOK, TOPK, E, CAP = 64, 2, 16, 12
PAIR = 2 * CAP
ROWS = E * CAP
SEND = E * PAIR
DW = 256
F = 1792
H = F // NC
RX = ROWS // RING

ALONG_X = [[[(x * NY + y) * NC + c for x in range(NX)] for y in range(NY)] for c in range(NC)]
ALONG_Y = [[[(x * NY + y) * NC + c for y in range(NY)] for x in range(NX)] for c in range(NC)]
FIRST = ALONG_X[0] + ALONG_Y[1]
SECOND = ALONG_Y[0] + ALONG_X[1]
SWAP = [(i, i ^ 1) for i in range(NX * NY * NC)]
VMEM = pl.BlockSpec(memory_space=pltpu.VMEM)


def core():
    return lax.rem(lax.axis_index("dp"), NC)


def place_in_first():
    d = lax.axis_index("dp")
    x, y = lax.div(d, NY * NC), lax.rem(lax.div(d, NC), NY)
    return jnp.where(core() == 0, x, y)


def mm(a, b):
    return lax.dot_general(a, b, (((1,), (0,)), ((), ())), preferred_element_type=F32)


def mm_t(a, b):
    return lax.dot_general(a, b, (((1,), (1,)), ((), ())), preferred_element_type=F32)


def iota(shape, dim):
    return lax.broadcasted_iota(jnp.int32, shape, dim)


def onehot(cond):
    return jnp.where(cond, 1.0, 0.0).astype(BF16)


def call(kernel, out_shape, count, limit_mb=12, flops=0, nbytes=0, **kw):
    kw.setdefault("in_specs", [VMEM] * count)
    return pl.pallas_call(
        kernel,
        out_shape=out_shape,
        out_specs=jax.tree.map(lambda _: VMEM, out_shape),
        compiler_params=pltpu.CompilerParams(vmem_limit_bytes=limit_mb << 20),
        cost_estimate=pl.CostEstimate(flops=flops, bytes_accessed=nbytes, transcendentals=0),
        **kw,
    )


def turned(row, eye):
    return jnp.sum(jnp.where(eye, row, jnp.zeros_like(row)), axis=1, keepdims=True)


def half_columns(c):
    return pl.ds(pl.multiple_of(c * H, H), H), pl.ds(pl.multiple_of(F + c * H, H), H)


def fetch_half(wgu_hbm, wd_hbm, wgu_ref, wd_ref, sems, c):
    gate, up = half_columns(c)
    return [
        pltpu.make_async_copy(wgu_hbm.at[:, gate], wgu_ref.at[:, pl.ds(0, H)], sems.at[0]),
        pltpu.make_async_copy(wgu_hbm.at[:, up], wgu_ref.at[:, pl.ds(H, H)], sems.at[1]),
        pltpu.make_async_copy(wd_hbm.at[gate, :], wd_ref, sems.at[2]),
    ]


def pack_kernel(
    ids_hbm, gate_hbm, tok_hbm, grad_hbm, wgu_hbm, wd_hbm,
    send_ref, place_ref, weight_ref, wgu_out, wd_out,
    ids_ref, gate_ref, tok_ref, grad_ref, sems, half_sems,
):
    pairs = [(ids_hbm, ids_ref), (gate_hbm, gate_ref), (tok_hbm, tok_ref), (grad_hbm, grad_ref)]
    moves = [pltpu.make_async_copy(*pair, sems.at[n]) for n, pair in enumerate(pairs)]
    moves += fetch_half(wgu_hbm, wd_hbm, wgu_out, wd_out, half_sems, 1 - core())
    for move in moves:
        move.start()
    eye = iota((TOK, TOK), 0) == iota((TOK, TOK), 1)
    before = onehot(iota((TOK, TOK), 0) < iota((TOK, TOK), 1))
    row = iota((SEND, TOK), 0)
    moves[0].wait()
    moves[1].wait()
    ids = ids_ref[...]
    hots = [(ids[k : k + 1, :] == iota((E, TOK), 0)).astype(F32) for k in range(TOPK)]
    earlier = mm((hots[0] + hots[1]).astype(BF16), before)
    across, places, weights = [], [], []
    for k in range(TOPK):
        rank = jnp.sum(hots[k] * earlier, axis=0, keepdims=True).astype(jnp.int32)
        place = ids[k : k + 1, :] * PAIR + rank
        across.append(place)
        places.append(turned(place, eye))
        weights.append(turned(gate_ref[k : k + 1, :], eye))
    place_ref[...] = jnp.concatenate(places, axis=1)
    weight_ref[...] = jnp.concatenate(weights, axis=1)
    moves[2].wait()
    pick_tok = onehot((row == across[0]) | (row == across[1]))
    total = mm(pick_tok, tok_ref[...])
    moves[3].wait()
    grad = grad_ref[...].astype(F32)
    for k in range(TOPK):
        total += mm(onehot(row == across[k] + CAP), (weights[k] * grad).astype(BF16))
    send_ref[...] = total.astype(BF16)
    for move in moves[4:]:
        move.wait()


def slot_to_pair(slot):
    extra = jnp.zeros_like(slot)
    for b in range(1, E):
        extra += jnp.where(slot >= b * CAP, CAP, 0)
    return slot + extra


def partials(x, g, wgu_ref, wd_ref):
    return mm(x, wgu_ref[:, :H]), mm(x, wgu_ref[:, H:]), mm_t(g, wd_ref[...])


def away_kernel(arr_ref, wgu_ref, wd_ref, out_ref, x_ref, g_ref):
    arrived = arr_ref[...]
    source = slot_to_pair(iota((ROWS, 1), 0))
    col = iota((ROWS, SEND), 1)
    x_ref[...] = mm(onehot(col == source), arrived).astype(BF16)
    g_ref[...] = mm(onehot(col == source + CAP), arrived).astype(BF16)
    terms = partials(x_ref[...], g_ref[...], wgu_ref, wd_ref)
    for j, term in enumerate(terms):
        out_ref[:, j * H : (j + 1) * H] = term.astype(BF16)


def home_kernel(x_ref, g_ref, wgu_hbm, wd_hbm, out_ref, wgu_out, wd_out, half_sems):
    moves = fetch_half(wgu_hbm, wd_hbm, wgu_out, wd_out, half_sems, core())
    for move in moves:
        move.start()
    for move in moves:
        move.wait()
    terms = partials(x_ref[...], g_ref[...], wgu_out, wd_out)
    for j, term in enumerate(terms):
        out_ref[:, j * H : (j + 1) * H] = term


def add_kernel(home_ref, got_ref, out_ref, own_ref):
    out_ref[...] = (home_ref[...] + got_ref[...].astype(F32)).astype(BF16)
    rows = pl.ds(pl.multiple_of(place_in_first() * RX, RX), RX)
    own_ref[...] = home_ref[rows, :] + got_ref[rows, :].astype(F32)


def sum_kernel(got_ref, own_ref, out_ref, rest_ref):
    i = place_in_first()
    total = own_ref[...] - got_ref[i].astype(F32)
    for j in range(RING):
        total += got_ref[j].astype(F32)
    rounded = total.astype(BF16)
    out_ref[0] = rounded
    rest_ref[...] = total - rounded.astype(F32)


def act_kernel(part_ref, rest_ref, out_ref):
    total = rest_ref[...]
    for i in range(RING):
        total += part_ref[i].astype(F32)
    gate, up, hg = total[:, :H], total[:, H : 2 * H], total[:, 2 * H :]
    sig = jax.nn.sigmoid(gate)
    silu = gate * sig
    out_ref[0, :, :H] = (silu * up).astype(BF16)
    out_ref[0, :, H : 2 * H] = (hg * up * sig * (1.0 + gate * (1.0 - sig))).astype(BF16)
    out_ref[0, :, 2 * H :] = (hg * silu).astype(BF16)


def products(act_ref, wgu_ref, wd_ref):
    back = mm_t(act_ref[:, H : 2 * H], wgu_ref[:, :H]) + mm_t(act_ref[:, 2 * H :], wgu_ref[:, H:])
    return mm(act_ref[:, :H], wd_ref[...]), back


def first_kernel(act_ref, wgu_ref, wd_ref, place_ref, out_ref, back_ref, spread_ref, pick_ref):
    out_ref[...], back_ref[...] = products(act_ref, wgu_ref, wd_ref)
    row = iota((SEND, ROWS), 0)
    target = slot_to_pair(iota((1, ROWS), 1))
    spread_ref[:, :ROWS] = onehot(row == target)
    spread_ref[:, ROWS:] = onehot(row == target + CAP)
    col = iota((TOK, SEND), 1)
    at = [place_ref[:, k : k + 1] for k in range(TOPK)]
    for k in range(TOPK):
        pick_ref[k * TOK : (k + 1) * TOK, :] = onehot(col == at[k])
    pick_ref[TOPK * TOK :, :] = onehot((col == at[0] + CAP) | (col == at[1] + CAP))


def finish_kernel(act_ref, wgu_ref, wd_ref, out_ref, back_ref, spread_ref, send_ref):
    out, back = products(act_ref, wgu_ref, wd_ref)
    rows = [(out_ref[...] + out).astype(BF16), (back_ref[...] + back).astype(BF16)]
    send_ref[...] = mm(spread_ref[...], jnp.concatenate(rows, axis=0)).astype(BF16)


def combine_kernel(ret_ref, weight_ref, pick_ref, moe_ref, tok_ref):
    picked = mm(pick_ref[...], ret_ref[...])
    moe = weight_ref[:, :1] * picked[:TOK]
    for k in range(1, TOPK):
        moe += weight_ref[:, k : k + 1] * picked[k * TOK : (k + 1) * TOK]
    moe_ref[...] = moe.astype(BF16)
    tok_ref[...] = picked[TOPK * TOK :].astype(BF16)


def local(tokens, gate_up, down, expert_ids, gate_values, out_grad):
    sds = jax.ShapeDtypeStruct
    wide16, wide32 = (sds((ROWS, 3 * H), t) for t in (BF16, F32))
    narrow16, narrow32 = (sds((ROWS, DW), t) for t in (BF16, F32))
    chunk16, chunk32 = sds((1, RX, 3 * H), BF16), sds((RX, 3 * H), F32)
    small = [pltpu.VMEM((TOPK, TOK), jnp.int32), pltpu.VMEM((TOPK, TOK), F32)]
    small += [pltpu.VMEM((TOK, DW), BF16)] * 2
    half = (sds((DW, 2 * H), BF16), sds((H, DW), BF16))
    hbm = pl.BlockSpec(memory_space=pltpu.HBM)
    in_hbm = lambda *vs: [pltpu.with_memory_space_constraint(v, pltpu.HBM) for v in vs]
    wgu, wd = in_hbm(gate_up[0], down[0])
    work = dict(flops=2 * ROWS * DW * 3 * H, nbytes=4 << 20)

    send, place, weight, wgu_away, wd_away = call(
        pack_kernel,
        (
            sds((SEND, DW), BF16),
            sds((TOK, TOPK), jnp.int32),
            sds((TOK, TOPK), F32),
            *half,
        ),
        6,
        in_specs=[hbm] * 6,
        scratch_shapes=small + [pltpu.SemaphoreType.DMA((n,)) for n in (4, 3)],
    )(*in_hbm(expert_ids.T, gate_values.T, tokens, out_grad), wgu, wd)
    arrived = lax.all_to_all(
        send.reshape(E, PAIR, DW), "expert", 0, 0, tiled=True
    ).reshape(SEND, DW)
    away, x, g = call(away_kernel, (wide16, narrow16, narrow16), 3, **work)(
        arrived, wgu_away, wd_away
    )
    got = lax.ppermute(away, "dp", SWAP)
    home, wgu_home, wd_home = call(
        home_kernel,
        (wide32, *half),
        4,
        in_specs=[VMEM, VMEM, hbm, hbm],
        scratch_shapes=[pltpu.SemaphoreType.DMA((3,))],
        **work,
    )(x, g, wgu, wd)
    chip, own = call(add_kernel, (wide16, chunk32), 2)(home, got)
    got = lax.all_to_all(
        chip.reshape(RING, RX, 3 * H), "dp", 0, 0, axis_index_groups=FIRST, tiled=True
    )
    chunk, rest = call(sum_kernel, (chunk16, chunk32), 2)(got, own)
    parts = lax.all_gather(chunk, "dp", axis=0, axis_index_groups=SECOND, tiled=True)
    act = call(act_kernel, chunk16, 2)(parts, rest)
    mine = lax.all_gather(act, "dp", axis=0, axis_index_groups=FIRST, tiled=True)
    mine = mine.reshape(ROWS, 3 * H)
    other = lax.ppermute(mine, "dp", SWAP)
    spread, pick = sds((SEND, 2 * ROWS), BF16), sds(((TOPK + 1) * TOK, SEND), BF16)
    out, back, spread, pick = call(first_kernel, (narrow32, narrow32, spread, pick), 4, **work)(
        mine, wgu_home, wd_home, place
    )
    back = call(finish_kernel, sds((SEND, DW), BF16), 6)(
        other, wgu_away, wd_away, out, back, spread
    )
    returned = lax.all_to_all(
        back.reshape(E, PAIR, DW), "expert", 0, 0, tiled=True
    ).reshape(SEND, DW)
    shape = sds((TOK, DW), BF16)
    return call(combine_kernel, (shape, shape), 3)(returned, weight, pick)


def solution(mesh):
    rows, cols = P("expert", "dp"), P("expert", None)
    return jax.shard_map(
        local,
        mesh=mesh,
        in_specs=(rows, P("expert", "dp", None), P("expert", None, "dp"), cols, cols, rows),
        out_specs=(rows, rows),
        check_vma=False,
    )
```

```python
import jax
import jax.numpy as jnp
from jax import lax
from jax.experimental import pallas as pl
from jax.experimental.pallas import tpu as pltpu
from jax.sharding import PartitionSpec as P

BF16 = jnp.bfloat16
F32 = jnp.float32
NX, NY, NC = 4, 4, 2
RING = 4

TOK, TOPK, E, CAP = 64, 2, 16, 12
PAIR = 2 * CAP
ROWS = E * CAP
SEND = E * PAIR
DW = 256
F = 1792
H = F // NC
RX = ROWS // RING

ALONG_X = [[[(x * NY + y) * NC + c for x in range(NX)] for y in range(NY)] for c in range(NC)]
ALONG_Y = [[[(x * NY + y) * NC + c for y in range(NY)] for x in range(NX)] for c in range(NC)]
FIRST = ALONG_X[0] + ALONG_Y[1]
SECOND = ALONG_Y[0] + ALONG_X[1]
SWAP = [(i, i ^ 1) for i in range(NX * NY * NC)]
VMEM = pl.BlockSpec(memory_space=pltpu.VMEM)


def core():
    return lax.rem(lax.axis_index("dp"), NC)


def place_in_first():
    d = lax.axis_index("dp")
    x, y = lax.div(d, NY * NC), lax.rem(lax.div(d, NC), NY)
    return jnp.where(core() == 0, x, y)


def mm(a, b):
    return lax.dot_general(a, b, (((1,), (0,)), ((), ())), preferred_element_type=F32)


def mm_t(a, b):
    return lax.dot_general(a, b, (((1,), (1,)), ((), ())), preferred_element_type=F32)


def iota(shape, dim):
    return lax.broadcasted_iota(jnp.int32, shape, dim)


def onehot(cond):
    return jnp.where(cond, 1.0, 0.0).astype(BF16)


def call(kernel, out_shape, count, limit_mb=12, flops=0, nbytes=0, **kw):
    kw.setdefault("in_specs", [VMEM] * count)
    return pl.pallas_call(
        kernel,
        out_shape=out_shape,
        out_specs=jax.tree.map(lambda _: VMEM, out_shape),
        compiler_params=pltpu.CompilerParams(vmem_limit_bytes=limit_mb << 20),
        cost_estimate=pl.CostEstimate(flops=flops, bytes_accessed=nbytes, transcendentals=0),
        **kw,
    )


def turned(row, eye):
    return jnp.sum(jnp.where(eye, row, jnp.zeros_like(row)), axis=1, keepdims=True)


def half_columns(c):
    return pl.ds(pl.multiple_of(c * H, H), H), pl.ds(pl.multiple_of(F + c * H, H), H)


def fetch_half(wgu_hbm, wd_hbm, wgu_ref, wd_ref, sems, c):
    gate, up = half_columns(c)
    return [
        pltpu.make_async_copy(wgu_hbm.at[:, gate], wgu_ref.at[:, pl.ds(0, H)], sems.at[0]),
        pltpu.make_async_copy(wgu_hbm.at[:, up], wgu_ref.at[:, pl.ds(H, H)], sems.at[1]),
        pltpu.make_async_copy(wd_hbm.at[gate, :], wd_ref, sems.at[2]),
    ]


def pack_kernel(
    ids_hbm, gate_hbm, tok_hbm, grad_hbm, wgu_hbm, wd_hbm,
    send_ref, place_ref, weight_ref, wgu_out, wd_out,
    ids_ref, gate_ref, tok_ref, grad_ref, sems, half_sems,
):
    pairs = [(ids_hbm, ids_ref), (gate_hbm, gate_ref), (tok_hbm, tok_ref), (grad_hbm, grad_ref)]
    moves = [pltpu.make_async_copy(*pair, sems.at[n]) for n, pair in enumerate(pairs)]
    moves += fetch_half(wgu_hbm, wd_hbm, wgu_out, wd_out, half_sems, 1 - core())
    for move in moves:
        move.start()
    eye = iota((TOK, TOK), 0) == iota((TOK, TOK), 1)
    before = onehot(iota((TOK, TOK), 0) < iota((TOK, TOK), 1))
    moves[0].wait()
    moves[1].wait()
    ids = ids_ref[...]
    hots = [(ids[k : k + 1, :] == iota((E, TOK), 0)).astype(F32) for k in range(TOPK)]
    earlier = mm((hots[0] + hots[1]).astype(BF16), before)
    across, places, weights = [], [], []
    for k in range(TOPK):
        rank = jnp.sum(hots[k] * earlier, axis=0, keepdims=True).astype(jnp.int32)
        place = ids[k : k + 1, :] * PAIR + rank
        across.append(place)
        places.append(turned(place, eye))
        weights.append(turned(gate_ref[k : k + 1, :], eye))
    place_ref[...] = jnp.concatenate(places, axis=1)
    weight_ref[...] = jnp.concatenate(weights, axis=1)
    moves[2].wait()
    moves[3].wait()
    grad = grad_ref[...].astype(F32)
    values = [tok_ref[...]] + [(weights[k] * grad).astype(BF16) for k in range(TOPK)]
    first = jnp.concatenate(across[:1] + [at + CAP for at in across], axis=1)
    second = jnp.concatenate(across[1:2] + [at + CAP for at in across], axis=1)
    row = iota((SEND, TOK * (TOPK + 1)), 0)
    pick = onehot((row == first) | (row == second))
    total = mm(pick, jnp.concatenate(values, axis=0))
    send_ref[...] = total.astype(BF16)
    for move in moves[4:]:
        move.wait()


def partials(x, g, wgu_ref, wd_ref):
    return mm(x, wgu_ref[:, :H]), mm(x, wgu_ref[:, H:]), mm_t(g, wd_ref[...])


def away_kernel(arr_ref, wgu_ref, wd_ref, out_ref, x_ref, g_ref, pair_ref, sort_ref):
    pair_ref[...] = arr_ref[...].astype(F32)
    for n, rows_ref in enumerate((x_ref, g_ref)):
        for b in range(E):
            at = b * PAIR + n * CAP
            sort_ref[b * CAP : (b + 1) * CAP, :] = pair_ref[at : at + CAP, :]
        rows_ref[...] = sort_ref[...].astype(BF16)
    terms = partials(x_ref[...], g_ref[...], wgu_ref, wd_ref)
    for j, term in enumerate(terms):
        out_ref[:, j * H : (j + 1) * H] = term.astype(BF16)


def home_kernel(x_ref, g_ref, wgu_hbm, wd_hbm, out_ref, wgu_out, wd_out, half_sems):
    moves = fetch_half(wgu_hbm, wd_hbm, wgu_out, wd_out, half_sems, core())
    for move in moves:
        move.start()
    for move in moves:
        move.wait()
    terms = partials(x_ref[...], g_ref[...], wgu_out, wd_out)
    for j, term in enumerate(terms):
        out_ref[:, j * H : (j + 1) * H] = term


def add_kernel(home_ref, got_ref, out_ref, own_ref):
    out_ref[...] = (home_ref[...] + got_ref[...].astype(F32)).astype(BF16)
    rows = pl.ds(pl.multiple_of(place_in_first() * RX, RX), RX)
    own_ref[...] = home_ref[rows, :] + got_ref[rows, :].astype(F32)


def sum_kernel(got_ref, own_ref, out_ref, rest_ref):
    i = place_in_first()
    total = own_ref[...] - got_ref[i].astype(F32)
    for j in range(RING):
        total += got_ref[j].astype(F32)
    rounded = total.astype(BF16)
    out_ref[0] = rounded
    rest_ref[...] = total - rounded.astype(F32)


def act_kernel(part_ref, rest_ref, out_ref):
    total = rest_ref[...]
    for i in range(RING):
        total += part_ref[i].astype(F32)
    gate, up, hg = total[:, :H], total[:, H : 2 * H], total[:, 2 * H :]
    sig = jax.nn.sigmoid(gate)
    silu = gate * sig
    out_ref[0, :, :H] = (silu * up).astype(BF16)
    out_ref[0, :, H : 2 * H] = (hg * up * sig * (1.0 + gate * (1.0 - sig))).astype(BF16)
    out_ref[0, :, 2 * H :] = (hg * silu).astype(BF16)


def products(act_ref, wgu_ref, wd_ref):
    back = mm_t(act_ref[:, H : 2 * H], wgu_ref[:, :H]) + mm_t(act_ref[:, 2 * H :], wgu_ref[:, H:])
    return mm(act_ref[:, :H], wd_ref[...]), back


def first_kernel(act_ref, wgu_ref, wd_ref, place_ref, out_ref, back_ref, pick_ref):
    out_ref[...], back_ref[...] = products(act_ref, wgu_ref, wd_ref)
    col = iota((TOK, SEND), 1)
    at = [place_ref[:, k : k + 1] for k in range(TOPK)]
    for k in range(TOPK):
        pick_ref[k * TOK : (k + 1) * TOK, :] = onehot(col == at[k])
    pick_ref[TOPK * TOK :, :] = onehot((col == at[0] + CAP) | (col == at[1] + CAP))


def finish_kernel(act_ref, wgu_ref, wd_ref, out_ref, back_ref, send_ref, pair_ref, sort_ref):
    terms = products(act_ref, wgu_ref, wd_ref)
    for n, (own_ref, term) in enumerate(zip((out_ref, back_ref), terms)):
        sort_ref[...] = own_ref[...] + term
        for b in range(E):
            at = b * PAIR + n * CAP
            pair_ref[at : at + CAP, :] = sort_ref[b * CAP : (b + 1) * CAP, :]
    send_ref[...] = pair_ref[...].astype(BF16)


def combine_kernel(ret_ref, weight_ref, pick_ref, moe_ref, tok_ref):
    picked = mm(pick_ref[...], ret_ref[...])
    moe = weight_ref[:, :1] * picked[:TOK]
    for k in range(1, TOPK):
        moe += weight_ref[:, k : k + 1] * picked[k * TOK : (k + 1) * TOK]
    moe_ref[...] = moe.astype(BF16)
    tok_ref[...] = picked[TOPK * TOK :].astype(BF16)


def local(tokens, gate_up, down, expert_ids, gate_values, out_grad):
    sds = jax.ShapeDtypeStruct
    wide16, wide32 = (sds((ROWS, 3 * H), t) for t in (BF16, F32))
    narrow16, narrow32 = (sds((ROWS, DW), t) for t in (BF16, F32))
    chunk16, chunk32 = sds((1, RX, 3 * H), BF16), sds((RX, 3 * H), F32)
    small = [pltpu.VMEM((TOPK, TOK), jnp.int32), pltpu.VMEM((TOPK, TOK), F32)]
    small += [pltpu.VMEM((TOK, DW), BF16)] * 2
    half = (sds((DW, 2 * H), BF16), sds((H, DW), BF16))
    hbm = pl.BlockSpec(memory_space=pltpu.HBM)
    in_hbm = lambda *vs: [pltpu.with_memory_space_constraint(v, pltpu.HBM) for v in vs]
    wgu, wd = in_hbm(gate_up[0], down[0])
    work = dict(flops=2 * ROWS * DW * 3 * H, nbytes=4 << 20)

    send, place, weight, wgu_away, wd_away = call(
        pack_kernel,
        (
            sds((SEND, DW), BF16),
            sds((TOK, TOPK), jnp.int32),
            sds((TOK, TOPK), F32),
            *half,
        ),
        6,
        in_specs=[hbm] * 6,
        scratch_shapes=small + [pltpu.SemaphoreType.DMA((n,)) for n in (4, 3)],
    )(*in_hbm(expert_ids.T, gate_values.T, tokens, out_grad), wgu, wd)
    arrived = lax.all_to_all(
        send.reshape(E, PAIR, DW), "expert", 0, 0, tiled=True
    ).reshape(SEND, DW)
    away, x, g = call(
        away_kernel,
        (wide16, narrow16, narrow16),
        3,
        scratch_shapes=[pltpu.VMEM((SEND, DW), F32), pltpu.VMEM((ROWS, DW), F32)],
        **work,
    )(
        arrived, wgu_away, wd_away
    )
    got = lax.ppermute(away, "dp", SWAP)
    home, wgu_home, wd_home = call(
        home_kernel,
        (wide32, *half),
        4,
        in_specs=[VMEM, VMEM, hbm, hbm],
        scratch_shapes=[pltpu.SemaphoreType.DMA((3,))],
        **work,
    )(x, g, wgu, wd)
    chip, own = call(add_kernel, (wide16, chunk32), 2)(home, got)
    got = lax.all_to_all(
        chip.reshape(RING, RX, 3 * H), "dp", 0, 0, axis_index_groups=FIRST, tiled=True
    )
    chunk, rest = call(sum_kernel, (chunk16, chunk32), 2)(got, own)
    parts = lax.all_gather(chunk, "dp", axis=0, axis_index_groups=SECOND, tiled=True)
    act = call(act_kernel, chunk16, 2)(parts, rest)
    mine = lax.all_gather(act, "dp", axis=0, axis_index_groups=FIRST, tiled=True)
    mine = mine.reshape(ROWS, 3 * H)
    other = lax.ppermute(mine, "dp", SWAP)
    pick = sds(((TOPK + 1) * TOK, SEND), BF16)
    out, back, pick = call(first_kernel, (narrow32, narrow32, pick), 4, **work)(
        mine, wgu_home, wd_home, place
    )
    back = call(
        finish_kernel,
        sds((SEND, DW), BF16),
        5,
        scratch_shapes=[pltpu.VMEM((SEND, DW), F32), pltpu.VMEM((ROWS, DW), F32)],
    )(other, wgu_away, wd_away, out, back)
    returned = lax.all_to_all(
        back.reshape(E, PAIR, DW), "expert", 0, 0, tiled=True
    ).reshape(SEND, DW)
    shape = sds((TOK, DW), BF16)
    return call(combine_kernel, (shape, shape), 3)(returned, weight, pick)


def solution(mesh):
    rows, cols = P("expert", "dp"), P("expert", None)
    return jax.shard_map(
        local,
        mesh=mesh,
        in_specs=(rows, P("expert", "dp", None), P("expert", None, "dp"), cols, cols, rows),
        out_specs=(rows, rows),
        check_vma=False,
    )
```

```python
import jax
import jax.numpy as jnp
from jax import lax
from jax.experimental import pallas as pl
from jax.experimental.pallas import tpu as pltpu
from jax.sharding import PartitionSpec as P

BF16 = jnp.bfloat16
F32 = jnp.float32
NX, NY, NC = 4, 4, 2
RING = 4

TOK, TOPK, E, CAP = 64, 2, 16, 12
PAIR = 2 * CAP
ROWS = E * CAP
SEND = E * PAIR
DW = 256
F = 1792
H = F // NC
RX = ROWS // RING

ALONG_X = [[[(x * NY + y) * NC + c for x in range(NX)] for y in range(NY)] for c in range(NC)]
ALONG_Y = [[[(x * NY + y) * NC + c for y in range(NY)] for x in range(NX)] for c in range(NC)]
FIRST = ALONG_X[0] + ALONG_Y[1]
SECOND = ALONG_Y[0] + ALONG_X[1]
SWAP = [(i, i ^ 1) for i in range(NX * NY * NC)]
VMEM = pl.BlockSpec(memory_space=pltpu.VMEM)


def core():
    return lax.rem(lax.axis_index("dp"), NC)


def place_in_first():
    d = lax.axis_index("dp")
    x, y = lax.div(d, NY * NC), lax.rem(lax.div(d, NC), NY)
    return jnp.where(core() == 0, x, y)


def mm(a, b):
    return lax.dot_general(a, b, (((1,), (0,)), ((), ())), preferred_element_type=F32)


def mm_t(a, b):
    return lax.dot_general(a, b, (((1,), (1,)), ((), ())), preferred_element_type=F32)


def iota(shape, dim):
    return lax.broadcasted_iota(jnp.int32, shape, dim)


def onehot(cond):
    return jnp.where(cond, 1.0, 0.0).astype(BF16)


def call(kernel, out_shape, count, limit_mb=12, flops=0, nbytes=0, **kw):
    kw.setdefault("in_specs", [VMEM] * count)
    kw.setdefault("out_specs", jax.tree.map(lambda _: VMEM, out_shape))
    return pl.pallas_call(
        kernel,
        out_shape=out_shape,
        compiler_params=pltpu.CompilerParams(vmem_limit_bytes=limit_mb << 20),
        cost_estimate=pl.CostEstimate(flops=flops, bytes_accessed=nbytes, transcendentals=0),
        **kw,
    )


def turned(row, eye):
    return jnp.sum(jnp.where(eye, row, jnp.zeros_like(row)), axis=1, keepdims=True)


def half_columns(c):
    return pl.ds(pl.multiple_of(c * H, H), H), pl.ds(pl.multiple_of(F + c * H, H), H)


def fetch_half(wgu_hbm, wd_hbm, refs, sems, c):
    gate, up = half_columns(c)
    parts = (wgu_hbm.at[:, gate], wgu_hbm.at[:, up], wd_hbm.at[gate, :])
    return [pltpu.make_async_copy(p, r, sems.at[n]) for n, (p, r) in enumerate(zip(parts, refs))]


def pack_kernel(
    ids_hbm, gate_hbm, tok_hbm, grad_hbm, wgu_hbm, wd_hbm,
    send_hbm, place_ref, weight_ref, *refs,
):
    *weight_refs, ids_ref, gate_ref, tok_ref, grad_ref, send_ref, sems, half_sems = refs
    pairs = [(ids_hbm, ids_ref), (gate_hbm, gate_ref), (tok_hbm, tok_ref), (grad_hbm, grad_ref)]
    moves = [pltpu.make_async_copy(*pair, sems.at[n]) for n, pair in enumerate(pairs)]
    moves += fetch_half(wgu_hbm, wd_hbm, weight_refs[:3], half_sems, 1 - core())
    rows = pl.ds(pl.multiple_of(core() * H, H), H)
    moves.append(pltpu.make_async_copy(wd_hbm.at[rows, :], weight_refs[3], half_sems.at[3]))
    for move in moves:
        move.start()
    eye = iota((TOK, TOK), 0) == iota((TOK, TOK), 1)
    before = onehot(iota((TOK, TOK), 0) < iota((TOK, TOK), 1))
    moves[0].wait()
    moves[1].wait()
    ids = ids_ref[...]
    hots = [(ids[k : k + 1, :] == iota((E, TOK), 0)).astype(F32) for k in range(TOPK)]
    earlier = mm((hots[0] + hots[1]).astype(BF16), before)
    across, places, weights = [], [], []
    for k in range(TOPK):
        rank = jnp.sum(hots[k] * earlier, axis=0, keepdims=True).astype(jnp.int32)
        place = ids[k : k + 1, :] * PAIR + rank
        across.append(place)
        places.append(turned(place, eye))
        weights.append(turned(gate_ref[k : k + 1, :], eye))
    place_ref[...] = jnp.concatenate(places, axis=1)
    weight_ref[...] = jnp.concatenate(weights, axis=1)
    moves[2].wait()
    moves[3].wait()
    grad = grad_ref[...].astype(F32)
    values = [tok_ref[...]] + [(weights[k] * grad).astype(BF16) for k in range(TOPK)]
    first = jnp.concatenate(across[:1] + [at + CAP for at in across], axis=1)
    second = jnp.concatenate(across[1:2] + [at + CAP for at in across], axis=1)
    row = iota((SEND, TOK * (TOPK + 1)), 0)
    pick = onehot((row == first) | (row == second))
    total = mm(pick, jnp.concatenate(values, axis=0))
    send_ref[...] = total.astype(BF16)
    written = pltpu.make_async_copy(send_ref, send_hbm, sems.at[4])
    written.start()
    for move in moves[4:]:
        move.wait()
    written.wait()


def partials(rows_ref, gate_ref, up_ref, down_ref):
    x = rows_ref[:ROWS]
    return mm(x, gate_ref[...]), mm(x, up_ref[...]), mm_t(rows_ref[ROWS:], down_ref[...])


def sort_kernel(arr_ref, rows_ref, pair_ref, sort_ref):
    pair_ref[...] = arr_ref[...].astype(F32)
    for n in range(2):
        for b in range(E):
            at = b * PAIR + n * CAP
            sort_ref[b * CAP : (b + 1) * CAP, :] = pair_ref[at : at + CAP, :]
        rows_ref[n * ROWS : (n + 1) * ROWS] = sort_ref[...].astype(BF16)


def home_kernel(rows_ref, down_ref, wgu_hbm, out_ref, gate_ref, up_ref, sems):
    held = (gate_ref, up_ref)
    moves = [
        pltpu.make_async_copy(wgu_hbm.at[:, cols], ref, sems.at[n])
        for n, (cols, ref) in enumerate(zip(half_columns(core()), held))
    ]
    for move in moves:
        move.start()
    out_ref[:, 2 * H :] = mm_t(rows_ref[ROWS:], down_ref[...])
    for j, (move, w_ref) in enumerate(zip(moves, held)):
        move.wait()
        out_ref[:, j * H : (j + 1) * H] = mm(rows_ref[:ROWS], w_ref[...])


def join_kernel(home_ref, rows_ref, gate_ref, up_ref, down_ref, out_ref, own_ref, sum_ref):
    for j, term in enumerate(partials(rows_ref, gate_ref, up_ref, down_ref)):
        cols = slice(j * H, (j + 1) * H)
        sum_ref[:, cols] = home_ref[:, cols] + term
        out_ref[:, cols] = sum_ref[:, cols].astype(BF16)
    own_ref[...] = sum_ref[pl.ds(pl.multiple_of(place_in_first() * RX, RX), RX), :]


def sum_kernel(got_ref, own_ref, out_ref, rest_ref):
    i = place_in_first()
    total = own_ref[...] - got_ref[i].astype(F32)
    for j in range(RING):
        total += got_ref[j].astype(F32)
    rounded = total.astype(BF16)
    out_ref[0] = rounded
    rest_ref[...] = total - rounded.astype(F32)


def act_kernel(part_ref, rest_ref, out_ref):
    total = rest_ref[...]
    for i in range(RING):
        total += part_ref[i].astype(F32)
    gate, up, hg = total[:, :H], total[:, H : 2 * H], total[:, 2 * H :]
    sig = jax.nn.sigmoid(gate)
    silu = gate * sig
    out_ref[0, :, :H] = (silu * up).astype(BF16)
    out_ref[0, :, H : 2 * H] = (hg * up * sig * (1.0 + gate * (1.0 - sig))).astype(BF16)
    out_ref[0, :, 2 * H :] = (hg * silu).astype(BF16)


def products(act_ref, gate_ref, up_ref, down_ref):
    back = mm_t(act_ref[:, H : 2 * H], gate_ref[...]) + mm_t(act_ref[:, 2 * H :], up_ref[...])
    return mm(act_ref[:, :H], down_ref[...]), back


def other_kernel(act_ref, gate_ref, up_ref, down_ref, out_ref):
    out, back = products(act_ref, gate_ref, up_ref, down_ref)
    out_ref[:ROWS] = out.astype(BF16)
    out_ref[ROWS:] = back.astype(BF16)


def first_kernel(act_ref, gate_ref, up_ref, down_ref, place_ref, out_ref, pick_ref):
    out_ref[:ROWS], out_ref[ROWS:] = products(act_ref, gate_ref, up_ref, down_ref)
    col = iota((TOK, SEND), 1)
    at = [place_ref[:, k : k + 1] for k in range(TOPK)]
    for k in range(TOPK):
        pick_ref[k * TOK : (k + 1) * TOK, :] = onehot(col == at[k])
    pick_ref[TOPK * TOK :, :] = onehot((col == at[0] + CAP) | (col == at[1] + CAP))


def finish_kernel(own_ref, got_ref, send_ref, pair_ref, sort_ref):
    sort_ref[...] = own_ref[...] + got_ref[...].astype(F32)
    for n in range(2):
        for b in range(E):
            at = b * PAIR + n * CAP
            start = n * ROWS + b * CAP
            pair_ref[at : at + CAP, :] = sort_ref[start : start + CAP, :]
    send_ref[...] = pair_ref[...].astype(BF16)


def combine_kernel(ret_ref, weight_ref, pick_ref, moe_ref, tok_ref):
    picked = mm(pick_ref[...], ret_ref[...])
    moe = weight_ref[:, :1] * picked[:TOK]
    for k in range(1, TOPK):
        moe += weight_ref[:, k : k + 1] * picked[k * TOK : (k + 1) * TOK]
    moe_ref[...] = moe.astype(BF16)
    tok_ref[...] = picked[TOPK * TOK :].astype(BF16)


def local(tokens, gate_up, down, expert_ids, gate_values, out_grad):
    sds = jax.ShapeDtypeStruct
    wide16, wide32 = (sds((ROWS, 3 * H), t) for t in (BF16, F32))
    pair16, pair32 = (sds((SEND, DW), t) for t in (BF16, F32))
    chunk16, chunk32 = sds((1, RX, 3 * H), BF16), sds((RX, 3 * H), F32)
    half = (sds((DW, H), BF16), sds((DW, H), BF16), sds((H, DW), BF16))
    small = [pltpu.VMEM((TOPK, TOK), jnp.int32), pltpu.VMEM((TOPK, TOK), F32)]
    small += [pltpu.VMEM((TOK, DW), BF16)] * 2 + [pltpu.VMEM((SEND, DW), BF16)]
    sort = [pltpu.VMEM((SEND, DW), F32), pltpu.VMEM((ROWS, DW), F32)]
    hbm = pl.BlockSpec(memory_space=pltpu.HBM)
    in_hbm = lambda *vs: [pltpu.with_memory_space_constraint(v, pltpu.HBM) for v in vs]
    wgu, wd = in_hbm(gate_up[0], down[0])
    work = dict(flops=2 * ROWS * DW * 3 * H, nbytes=4 << 20)

    send, place, weight, *theirs, held_down = call(
        pack_kernel,
        (pair16, sds((TOK, TOPK), jnp.int32), sds((TOK, TOPK), F32), *half, half[2]),
        6,
        in_specs=[hbm] * 6,
        out_specs=(hbm, *[VMEM] * 6),
        scratch_shapes=small + [pltpu.SemaphoreType.DMA((n,)) for n in (5, 4)],
    )(*in_hbm(expert_ids.T, gate_values.T, tokens, out_grad), wgu, wd)
    cross = [lax.ppermute(w, "dp", SWAP) for w in theirs]
    arrived = lax.all_to_all(
        send.reshape(E, PAIR, DW), "expert", 0, 0, tiled=True
    ).reshape(SEND, DW)
    rows = call(sort_kernel, pair16, 1, scratch_shapes=sort)(arrived)
    other = lax.ppermute(rows, "dp", SWAP)
    home, *held = call(
        home_kernel,
        (wide32, *half[:2]),
        3,
        in_specs=[VMEM, VMEM, hbm],
        scratch_shapes=[pltpu.SemaphoreType.DMA((2,))],
        **work,
    )(rows, held_down, wgu)
    held.append(held_down)
    chip, own = call(
        join_kernel,
        (wide16, chunk32),
        5,
        limit_mb=16,
        scratch_shapes=[pltpu.VMEM((ROWS, 3 * H), F32)],
        **work,
    )(home, other, *cross)
    got = lax.all_to_all(
        chip.reshape(RING, RX, 3 * H), "dp", 0, 0, axis_index_groups=FIRST, tiled=True
    )
    chunk, rest = call(sum_kernel, (chunk16, chunk32), 2)(got, own)
    parts = lax.all_gather(chunk, "dp", axis=0, axis_index_groups=SECOND, tiled=True)
    act = call(act_kernel, chunk16, 2)(parts, rest)
    mine = lax.all_gather(act, "dp", axis=0, axis_index_groups=FIRST, tiled=True)
    mine = mine.reshape(ROWS, 3 * H)
    terms = call(other_kernel, pair16, 4, **work)(mine, *cross)
    got = lax.ppermute(terms, "dp", SWAP)
    pick = sds(((TOPK + 1) * TOK, SEND), BF16)
    terms, pick = call(first_kernel, (pair32, pick), 5, **work)(mine, *held, place)
    sort[1] = pltpu.VMEM((SEND, DW), F32)
    back = call(finish_kernel, pair16, 2, scratch_shapes=sort)(terms, got)
    returned = lax.all_to_all(
        back.reshape(E, PAIR, DW), "expert", 0, 0, tiled=True
    ).reshape(SEND, DW)
    shape = sds((TOK, DW), BF16)
    return call(combine_kernel, (shape, shape), 3)(returned, weight, pick)


def solution(mesh):
    rows, cols = P("expert", "dp"), P("expert", None)
    return jax.shard_map(
        local,
        mesh=mesh,
        in_specs=(rows, P("expert", "dp", None), P("expert", None, "dp"), cols, cols, rows),
        out_specs=(rows, rows),
        check_vma=False,
    )
```

```python
import jax
import jax.numpy as jnp
from jax import lax
from jax.experimental import pallas as pl
from jax.experimental.pallas import tpu as pltpu
from jax.sharding import PartitionSpec as P

BF16 = jnp.bfloat16
F32 = jnp.float32
NX, NY, NC = 4, 4, 2
RING = 4

TOK, TOPK, E, CAP = 64, 2, 16, 12
PAIR = 2 * CAP
ROWS = E * CAP
SEND = E * PAIR
DW = 256
F = 1792
H = F // NC
RX = ROWS // RING

ALONG_X = [[[(x * NY + y) * NC + c for x in range(NX)] for y in range(NY)] for c in range(NC)]
ALONG_Y = [[[(x * NY + y) * NC + c for y in range(NY)] for x in range(NX)] for c in range(NC)]
FIRST = ALONG_X[0] + ALONG_Y[1]
SECOND = ALONG_Y[0] + ALONG_X[1]
SWAP = [(i, i ^ 1) for i in range(NX * NY * NC)]
VMEM = pl.BlockSpec(memory_space=pltpu.VMEM)


def core():
    return lax.rem(lax.axis_index("dp"), NC)


def place_in_first():
    d = lax.axis_index("dp")
    x, y = lax.div(d, NY * NC), lax.rem(lax.div(d, NC), NY)
    return jnp.where(core() == 0, x, y)


def mm(a, b):
    return lax.dot_general(a, b, (((1,), (0,)), ((), ())), preferred_element_type=F32)


def mm_t(a, b):
    return lax.dot_general(a, b, (((1,), (1,)), ((), ())), preferred_element_type=F32)


def iota(shape, dim):
    return lax.broadcasted_iota(jnp.int32, shape, dim)


def onehot(cond):
    return jnp.where(cond, 1.0, 0.0).astype(BF16)


def call(kernel, out_shape, count, limit_mb=12, flops=0, nbytes=0, **kw):
    kw.setdefault("in_specs", [VMEM] * count)
    kw.setdefault("out_specs", jax.tree.map(lambda _: VMEM, out_shape))
    return pl.pallas_call(
        kernel,
        out_shape=out_shape,
        compiler_params=pltpu.CompilerParams(vmem_limit_bytes=limit_mb << 20),
        cost_estimate=pl.CostEstimate(flops=flops, bytes_accessed=nbytes, transcendentals=0),
        **kw,
    )


def turned(row, eye):
    return jnp.sum(jnp.where(eye, row, jnp.zeros_like(row)), axis=1, keepdims=True)


def half_columns(c):
    return pl.ds(pl.multiple_of(c * H, H), H), pl.ds(pl.multiple_of(F + c * H, H), H)


def fetch_half(wgu_hbm, wd_hbm, refs, sems, c):
    gate, up = half_columns(c)
    parts = (wgu_hbm.at[:, gate], wgu_hbm.at[:, up], wd_hbm.at[gate, :])
    return [pltpu.make_async_copy(p, r, sems.at[n]) for n, (p, r) in enumerate(zip(parts, refs))]


def pack_kernel(
    ids_hbm, gate_hbm, tok_hbm, grad_hbm, wgu_hbm, wd_hbm,
    send_hbm, place_ref, weight_ref, *refs,
):
    *weight_refs, ids_ref, gate_ref, tok_ref, grad_ref, send_ref, sems, half_sems = refs
    pairs = [(ids_hbm, ids_ref), (gate_hbm, gate_ref), (tok_hbm, tok_ref), (grad_hbm, grad_ref)]
    moves = [pltpu.make_async_copy(*pair, sems.at[n]) for n, pair in enumerate(pairs)]
    moves += fetch_half(wgu_hbm, wd_hbm, weight_refs[:3], half_sems, 1 - core())
    rows = pl.ds(pl.multiple_of(core() * H, H), H)
    moves.append(pltpu.make_async_copy(wd_hbm.at[rows, :], weight_refs[3], half_sems.at[3]))
    for move in moves:
        move.start()
    eye = iota((TOK, TOK), 0) == iota((TOK, TOK), 1)
    before = onehot(iota((TOK, TOK), 0) < iota((TOK, TOK), 1))
    moves[0].wait()
    moves[1].wait()
    ids = ids_ref[...]
    hots = [(ids[k : k + 1, :] == iota((E, TOK), 0)).astype(F32) for k in range(TOPK)]
    earlier = mm((hots[0] + hots[1]).astype(BF16), before)
    across, weights = [], []
    for k in range(TOPK):
        rank = jnp.sum(hots[k] * earlier, axis=0, keepdims=True).astype(jnp.int32)
        place = ids[k : k + 1, :] * PAIR + rank
        across.append(place)
        weights.append(turned(gate_ref[k : k + 1, :], eye))
    weight_ref[...] = jnp.concatenate(weights, axis=1)
    moves[2].wait()
    moves[3].wait()
    grad = grad_ref[...].astype(F32)
    values = [tok_ref[...]] + [(weights[k] * grad).astype(BF16) for k in range(TOPK)]
    first = jnp.concatenate(across[:1] + [at + CAP for at in across], axis=1)
    second = jnp.concatenate(across[1:2] + [at + CAP for at in across], axis=1)
    row = iota((SEND, TOK * (TOPK + 1)), 0)
    pick = onehot((row == first) | (row == second))
    values = jnp.concatenate(values, axis=0)
    written = []
    for n in range(2):
        rows = pl.ds(n * (SEND // 2), SEND // 2)
        send_ref[rows, :] = mm(pick[n * (SEND // 2) : (n + 1) * (SEND // 2)], values).astype(BF16)
        written.append(
            pltpu.make_async_copy(send_ref.at[rows, :], send_hbm.at[rows, :], sems.at[4 + n])
        )
        written[n].start()
    place_ref[...] = jnp.concatenate([turned(place, eye) for place in across], axis=1)
    for move in moves[4:]:
        move.wait()
    for move in written:
        move.wait()


def partials(rows_ref, gate_ref, up_ref, down_ref):
    x = rows_ref[:ROWS]
    return mm(x, gate_ref[...]), mm(x, up_ref[...]), mm_t(rows_ref[ROWS:], down_ref[...])


def sort_kernel(arr_ref, rows_ref, pair_ref, sort_ref):
    pair_ref[...] = arr_ref[...].astype(F32)
    for n in range(2):
        for b in range(E):
            at = b * PAIR + n * CAP
            sort_ref[b * CAP : (b + 1) * CAP, :] = pair_ref[at : at + CAP, :]
        rows_ref[n * ROWS : (n + 1) * ROWS] = sort_ref[...].astype(BF16)


def home_kernel(rows_ref, down_ref, wgu_hbm, out_ref, gate_ref, up_ref, sems):
    held = (gate_ref, up_ref)
    moves = [
        pltpu.make_async_copy(wgu_hbm.at[:, cols], ref, sems.at[n])
        for n, (cols, ref) in enumerate(zip(half_columns(core()), held))
    ]
    for move in moves:
        move.start()
    out_ref[:, 2 * H :] = mm_t(rows_ref[ROWS:], down_ref[...])
    for j, (move, w_ref) in enumerate(zip(moves, held)):
        move.wait()
        out_ref[:, j * H : (j + 1) * H] = mm(rows_ref[:ROWS], w_ref[...])


def join_kernel(home_ref, rows_ref, gate_ref, up_ref, down_ref, out_ref, own_ref, sum_ref):
    for j, term in enumerate(partials(rows_ref, gate_ref, up_ref, down_ref)):
        cols = slice(j * H, (j + 1) * H)
        sum_ref[:, cols] = home_ref[:, cols] + term
        out_ref[:, cols] = sum_ref[:, cols].astype(BF16)
    own_ref[...] = sum_ref[pl.ds(pl.multiple_of(place_in_first() * RX, RX), RX), :]


def sum_kernel(got_ref, own_ref, out_ref, rest_ref):
    i = place_in_first()
    total = own_ref[...] - got_ref[i].astype(F32)
    for j in range(RING):
        total += got_ref[j].astype(F32)
    rounded = total.astype(BF16)
    out_ref[0] = rounded
    rest_ref[...] = total - rounded.astype(F32)


def act_kernel(part_ref, rest_ref, out_ref):
    total = rest_ref[...]
    for i in range(RING):
        total += part_ref[i].astype(F32)
    gate, up, hg = total[:, :H], total[:, H : 2 * H], total[:, 2 * H :]
    sig = jax.nn.sigmoid(gate)
    silu = gate * sig
    out_ref[0, :, :H] = (silu * up).astype(BF16)
    out_ref[0, :, H : 2 * H] = (hg * up * sig * (1.0 + gate * (1.0 - sig))).astype(BF16)
    out_ref[0, :, 2 * H :] = (hg * silu).astype(BF16)


def products(act_ref, gate_ref, up_ref, down_ref):
    back = mm_t(act_ref[:, H : 2 * H], gate_ref[...]) + mm_t(act_ref[:, 2 * H :], up_ref[...])
    return mm(act_ref[:, :H], down_ref[...]), back


def other_kernel(act_ref, gate_ref, up_ref, down_ref, out_ref):
    out, back = products(act_ref, gate_ref, up_ref, down_ref)
    out_ref[:ROWS] = out.astype(BF16)
    out_ref[ROWS:] = back.astype(BF16)


def first_kernel(act_ref, gate_ref, up_ref, down_ref, place_ref, out_ref, pick_ref):
    out_ref[:ROWS], out_ref[ROWS:] = products(act_ref, gate_ref, up_ref, down_ref)
    col = iota((TOK, SEND), 1)
    at = [place_ref[:, k : k + 1] for k in range(TOPK)]
    for k in range(TOPK):
        pick_ref[k * TOK : (k + 1) * TOK, :] = onehot(col == at[k])
    pick_ref[TOPK * TOK :, :] = onehot((col == at[0] + CAP) | (col == at[1] + CAP))


def finish_kernel(own_ref, got_ref, send_ref, pair_ref, sort_ref):
    sort_ref[...] = own_ref[...] + got_ref[...].astype(F32)
    for n in range(2):
        for b in range(E):
            at = b * PAIR + n * CAP
            start = n * ROWS + b * CAP
            pair_ref[at : at + CAP, :] = sort_ref[start : start + CAP, :]
    send_ref[...] = pair_ref[...].astype(BF16)


def combine_kernel(ret_ref, weight_ref, pick_ref, moe_ref, tok_ref):
    picked = mm(pick_ref[...], ret_ref[...])
    moe = weight_ref[:, :1] * picked[:TOK]
    for k in range(1, TOPK):
        moe += weight_ref[:, k : k + 1] * picked[k * TOK : (k + 1) * TOK]
    moe_ref[...] = moe.astype(BF16)
    tok_ref[...] = picked[TOPK * TOK :].astype(BF16)


def local(tokens, gate_up, down, expert_ids, gate_values, out_grad):
    sds = jax.ShapeDtypeStruct
    wide16, wide32 = (sds((ROWS, 3 * H), t) for t in (BF16, F32))
    pair16, pair32 = (sds((SEND, DW), t) for t in (BF16, F32))
    chunk16, chunk32 = sds((1, RX, 3 * H), BF16), sds((RX, 3 * H), F32)
    half = (sds((DW, H), BF16), sds((DW, H), BF16), sds((H, DW), BF16))
    small = [pltpu.VMEM((TOPK, TOK), jnp.int32), pltpu.VMEM((TOPK, TOK), F32)]
    small += [pltpu.VMEM((TOK, DW), BF16)] * 2 + [pltpu.VMEM((SEND, DW), BF16)]
    sort = [pltpu.VMEM((SEND, DW), F32), pltpu.VMEM((ROWS, DW), F32)]
    hbm = pl.BlockSpec(memory_space=pltpu.HBM)
    in_hbm = lambda *vs: [pltpu.with_memory_space_constraint(v, pltpu.HBM) for v in vs]
    wgu, wd = in_hbm(gate_up[0], down[0])
    work = dict(flops=2 * ROWS * DW * 3 * H, nbytes=4 << 20)

    send, place, weight, *theirs, held_down = call(
        pack_kernel,
        (pair16, sds((TOK, TOPK), jnp.int32), sds((TOK, TOPK), F32), *half, half[2]),
        6,
        in_specs=[hbm] * 6,
        out_specs=(hbm, *[VMEM] * 6),
        scratch_shapes=small + [pltpu.SemaphoreType.DMA((n,)) for n in (6, 4)],
    )(*in_hbm(expert_ids.T, gate_values.T, tokens, out_grad), wgu, wd)
    cross = [lax.ppermute(w, "dp", SWAP) for w in theirs]
    arrived = lax.all_to_all(
        send.reshape(E, PAIR, DW), "expert", 0, 0, tiled=True
    ).reshape(SEND, DW)
    rows = call(sort_kernel, pair16, 1, scratch_shapes=sort)(arrived)
    other = lax.ppermute(rows, "dp", SWAP)
    home, *held = call(
        home_kernel,
        (wide32, *half[:2]),
        3,
        in_specs=[VMEM, VMEM, hbm],
        scratch_shapes=[pltpu.SemaphoreType.DMA((2,))],
        **work,
    )(rows, held_down, wgu)
    held.append(held_down)
    chip, own = call(
        join_kernel,
        (wide16, chunk32),
        5,
        limit_mb=16,
        scratch_shapes=[pltpu.VMEM((ROWS, 3 * H), F32)],
        **work,
    )(home, other, *cross)
    got = lax.all_to_all(
        chip.reshape(RING, RX, 3 * H), "dp", 0, 0, axis_index_groups=FIRST, tiled=True
    )
    chunk, rest = call(sum_kernel, (chunk16, chunk32), 2)(got, own)
    parts = lax.all_gather(chunk, "dp", axis=0, axis_index_groups=SECOND, tiled=True)
    act = call(act_kernel, chunk16, 2)(parts, rest)
    mine = lax.all_gather(act, "dp", axis=0, axis_index_groups=FIRST, tiled=True)
    mine = mine.reshape(ROWS, 3 * H)
    terms = call(other_kernel, pair16, 4, **work)(mine, *cross)
    got = lax.ppermute(terms, "dp", SWAP)
    pick = sds(((TOPK + 1) * TOK, SEND), BF16)
    terms, pick = call(first_kernel, (pair32, pick), 5, **work)(mine, *held, place)
    sort[1] = pltpu.VMEM((SEND, DW), F32)
    back = call(finish_kernel, pair16, 2, scratch_shapes=sort)(terms, got)
    returned = lax.all_to_all(
        back.reshape(E, PAIR, DW), "expert", 0, 0, tiled=True
    ).reshape(SEND, DW)
    shape = sds((TOK, DW), BF16)
    return call(combine_kernel, (shape, shape), 3)(returned, weight, pick)


def solution(mesh):
    rows, cols = P("expert", "dp"), P("expert", None)
    return jax.shard_map(
        local,
        mesh=mesh,
        in_specs=(rows, P("expert", "dp", None), P("expert", None, "dp"), cols, cols, rows),
        out_specs=(rows, rows),
        check_vma=False,
    )
```

```python
import jax
import jax.numpy as jnp
from jax import lax
from jax.experimental import pallas as pl
from jax.experimental.pallas import tpu as pltpu
from jax.sharding import PartitionSpec as P

BF16 = jnp.bfloat16
F32 = jnp.float32
NX, NY, NC = 4, 4, 2
RING = 4

TOK, TOPK, E, CAP = 64, 2, 16, 12
PAIR = 2 * CAP
ROWS = E * CAP
SEND = E * PAIR
DW = 256
F = 1792
H = F // NC
RX = ROWS // RING

ALONG_X = [[[(x * NY + y) * NC + c for x in range(NX)] for y in range(NY)] for c in range(NC)]
ALONG_Y = [[[(x * NY + y) * NC + c for y in range(NY)] for x in range(NX)] for c in range(NC)]
FIRST = ALONG_X[0] + ALONG_Y[1]
SECOND = ALONG_Y[0] + ALONG_X[1]
SWAP = [(i, i ^ 1) for i in range(NX * NY * NC)]
VMEM = pl.BlockSpec(memory_space=pltpu.VMEM)


def core():
    return lax.rem(lax.axis_index("dp"), NC)


def place_in_first():
    d = lax.axis_index("dp")
    x, y = lax.div(d, NY * NC), lax.rem(lax.div(d, NC), NY)
    return jnp.where(core() == 0, x, y)


def mm(a, b):
    return lax.dot_general(a, b, (((1,), (0,)), ((), ())), preferred_element_type=F32)


def mm_t(a, b):
    return lax.dot_general(a, b, (((1,), (1,)), ((), ())), preferred_element_type=F32)


def iota(shape, dim):
    return lax.broadcasted_iota(jnp.int32, shape, dim)


def onehot(cond):
    return jnp.where(cond, 1.0, 0.0).astype(BF16)


def call(kernel, out_shape, count, limit_mb=12, flops=0, nbytes=0, **kw):
    kw.setdefault("in_specs", [VMEM] * count)
    kw.setdefault("out_specs", jax.tree.map(lambda _: VMEM, out_shape))
    return pl.pallas_call(
        kernel,
        out_shape=out_shape,
        compiler_params=pltpu.CompilerParams(vmem_limit_bytes=limit_mb << 20),
        cost_estimate=pl.CostEstimate(flops=flops, bytes_accessed=nbytes, transcendentals=0),
        **kw,
    )


def turned(row, eye):
    return jnp.sum(jnp.where(eye, row, jnp.zeros_like(row)), axis=1, keepdims=True)


def half_columns(c):
    return pl.ds(pl.multiple_of(c * H, H), H), pl.ds(pl.multiple_of(F + c * H, H), H)


def fetch_half(wgu_hbm, wd_hbm, refs, sems, c):
    gate, up = half_columns(c)
    parts = (wgu_hbm.at[:, gate], wgu_hbm.at[:, up], wd_hbm.at[gate, :])
    return [pltpu.make_async_copy(p, r, sems.at[n]) for n, (p, r) in enumerate(zip(parts, refs))]


def pack_kernel(
    ids_hbm, gate_hbm, tok_hbm, grad_hbm, wgu_hbm, wd_hbm,
    send_hbm, place_ref, weight_ref, *refs,
):
    *weight_refs, ids_ref, gate_ref, tok_ref, grad_ref, send_ref, sems, half_sems = refs
    pairs = [(ids_hbm, ids_ref), (gate_hbm, gate_ref), (tok_hbm, tok_ref), (grad_hbm, grad_ref)]
    moves = [pltpu.make_async_copy(*pair, sems.at[n]) for n, pair in enumerate(pairs)]
    moves += fetch_half(wgu_hbm, wd_hbm, weight_refs[:3], half_sems, 1 - core())
    rows = pl.ds(pl.multiple_of(core() * H, H), H)
    moves.append(pltpu.make_async_copy(wd_hbm.at[rows, :], weight_refs[3], half_sems.at[3]))
    for move in moves:
        move.start()
    eye = iota((TOK, TOK), 0) == iota((TOK, TOK), 1)
    before = onehot(iota((TOK, TOK), 0) < iota((TOK, TOK), 1))
    moves[0].wait()
    moves[1].wait()
    ids = ids_ref[...]
    hots = [(ids[k : k + 1, :] == iota((E, TOK), 0)).astype(F32) for k in range(TOPK)]
    earlier = mm((hots[0] + hots[1]).astype(BF16), before)
    across, weights = [], []
    for k in range(TOPK):
        rank = jnp.sum(hots[k] * earlier, axis=0, keepdims=True).astype(jnp.int32)
        place = ids[k : k + 1, :] * PAIR + rank
        across.append(place)
        weights.append(turned(gate_ref[k : k + 1, :], eye))
    weight_ref[...] = jnp.concatenate(weights, axis=1)
    moves[2].wait()
    moves[3].wait()
    grad = grad_ref[...].astype(F32)
    values = [tok_ref[...]] + [(weights[k] * grad).astype(BF16) for k in range(TOPK)]
    first = jnp.concatenate(across[:1] + [at + CAP for at in across], axis=1)
    second = jnp.concatenate(across[1:2] + [at + CAP for at in across], axis=1)
    row = iota((SEND, TOK * (TOPK + 1)), 0)
    pick = onehot((row == first) | (row == second))
    values = jnp.concatenate(values, axis=0)
    written = []
    for n in range(2):
        rows = pl.ds(n * (SEND // 2), SEND // 2)
        send_ref[rows, :] = mm(pick[n * (SEND // 2) : (n + 1) * (SEND // 2)], values).astype(BF16)
        written.append(
            pltpu.make_async_copy(send_ref.at[rows, :], send_hbm.at[rows, :], sems.at[4 + n])
        )
        written[n].start()
    place_ref[...] = jnp.concatenate([turned(place, eye) for place in across], axis=1)
    for move in moves[4:]:
        move.wait()
    for move in written:
        move.wait()


def partials(rows_ref, gate_ref, up_ref, down_ref):
    x = rows_ref[:ROWS]
    return mm(x, gate_ref[...]), mm(x, up_ref[...]), mm_t(rows_ref[ROWS:], down_ref[...])


def sort_kernel(arr_ref, rows_ref, pair_ref, sort_ref):
    pair_ref[...] = arr_ref[...].astype(F32)
    for n in range(2):
        for b in range(E):
            at = b * PAIR + n * CAP
            sort_ref[b * CAP : (b + 1) * CAP, :] = pair_ref[at : at + CAP, :]
        rows_ref[n * ROWS : (n + 1) * ROWS] = sort_ref[...].astype(BF16)


def home_kernel(rows_ref, down_ref, wgu_hbm, out_ref, gate_ref, up_ref, sems):
    held = (gate_ref, up_ref)
    moves = [
        pltpu.make_async_copy(wgu_hbm.at[:, cols], ref, sems.at[n])
        for n, (cols, ref) in enumerate(zip(half_columns(core()), held))
    ]
    for move in moves:
        move.start()
    out_ref[:, 2 * H :] = mm_t(rows_ref[ROWS:], down_ref[...])
    for j, (move, w_ref) in enumerate(zip(moves, held)):
        move.wait()
        out_ref[:, j * H : (j + 1) * H] = mm(rows_ref[:ROWS], w_ref[...])


def join_kernel(home_ref, rows_ref, gate_ref, up_ref, down_ref, out_ref):
    for j, term in enumerate(partials(rows_ref, gate_ref, up_ref, down_ref)):
        cols = slice(j * H, (j + 1) * H)
        out_ref[:, cols] = (home_ref[:, cols] + term).astype(BF16)


def sum_kernel(got_ref, out_ref):
    total = got_ref[0].astype(F32)
    for j in range(1, RING):
        total += got_ref[j].astype(F32)
    out_ref[0] = total.astype(BF16)


def act_kernel(part_ref, out_ref):
    total = part_ref[0].astype(F32)
    for i in range(1, RING):
        total += part_ref[i].astype(F32)
    gate, up, hg = total[:, :H], total[:, H : 2 * H], total[:, 2 * H :]
    sig = jax.nn.sigmoid(gate)
    silu = gate * sig
    out_ref[0, :, :H] = (silu * up).astype(BF16)
    out_ref[0, :, H : 2 * H] = (hg * up * sig * (1.0 + gate * (1.0 - sig))).astype(BF16)
    out_ref[0, :, 2 * H :] = (hg * silu).astype(BF16)


def products(act_ref, gate_ref, up_ref, down_ref):
    back = mm_t(act_ref[:, H : 2 * H], gate_ref[...]) + mm_t(act_ref[:, 2 * H :], up_ref[...])
    return mm(act_ref[:, :H], down_ref[...]), back


def other_kernel(act_ref, gate_ref, up_ref, down_ref, out_ref):
    out, back = products(act_ref, gate_ref, up_ref, down_ref)
    out_ref[:ROWS] = out.astype(BF16)
    out_ref[ROWS:] = back.astype(BF16)


def first_kernel(act_ref, gate_ref, up_ref, down_ref, place_ref, out_ref, pick_ref):
    out_ref[:ROWS], out_ref[ROWS:] = products(act_ref, gate_ref, up_ref, down_ref)
    col = iota((TOK, SEND), 1)
    at = [place_ref[:, k : k + 1] for k in range(TOPK)]
    for k in range(TOPK):
        pick_ref[k * TOK : (k + 1) * TOK, :] = onehot(col == at[k])
    pick_ref[TOPK * TOK :, :] = onehot((col == at[0] + CAP) | (col == at[1] + CAP))


def finish_kernel(own_ref, got_ref, send_ref, pair_ref, sort_ref):
    sort_ref[...] = own_ref[...] + got_ref[...].astype(F32)
    for n in range(2):
        for b in range(E):
            at = b * PAIR + n * CAP
            start = n * ROWS + b * CAP
            pair_ref[at : at + CAP, :] = sort_ref[start : start + CAP, :]
    send_ref[...] = pair_ref[...].astype(BF16)


def combine_kernel(ret_ref, weight_ref, pick_ref, moe_ref, tok_ref):
    picked = mm(pick_ref[...], ret_ref[...])
    moe = weight_ref[:, :1] * picked[:TOK]
    for k in range(1, TOPK):
        moe += weight_ref[:, k : k + 1] * picked[k * TOK : (k + 1) * TOK]
    moe_ref[...] = moe.astype(BF16)
    tok_ref[...] = picked[TOPK * TOK :].astype(BF16)


def local(tokens, gate_up, down, expert_ids, gate_values, out_grad):
    sds = jax.ShapeDtypeStruct
    wide16, wide32 = (sds((ROWS, 3 * H), t) for t in (BF16, F32))
    pair16, pair32 = (sds((SEND, DW), t) for t in (BF16, F32))
    chunk16, chunk32 = sds((1, RX, 3 * H), BF16), sds((RX, 3 * H), F32)
    half = (sds((DW, H), BF16), sds((DW, H), BF16), sds((H, DW), BF16))
    small = [pltpu.VMEM((TOPK, TOK), jnp.int32), pltpu.VMEM((TOPK, TOK), F32)]
    small += [pltpu.VMEM((TOK, DW), BF16)] * 2 + [pltpu.VMEM((SEND, DW), BF16)]
    sort = [pltpu.VMEM((SEND, DW), F32), pltpu.VMEM((ROWS, DW), F32)]
    hbm = pl.BlockSpec(memory_space=pltpu.HBM)
    in_hbm = lambda *vs: [pltpu.with_memory_space_constraint(v, pltpu.HBM) for v in vs]
    wgu, wd = in_hbm(gate_up[0], down[0])
    work = dict(flops=2 * ROWS * DW * 3 * H, nbytes=4 << 20)

    send, place, weight, *theirs, held_down = call(
        pack_kernel,
        (pair16, sds((TOK, TOPK), jnp.int32), sds((TOK, TOPK), F32), *half, half[2]),
        6,
        in_specs=[hbm] * 6,
        out_specs=(hbm, *[VMEM] * 6),
        scratch_shapes=small + [pltpu.SemaphoreType.DMA((n,)) for n in (6, 4)],
    )(*in_hbm(expert_ids.T, gate_values.T, tokens, out_grad), wgu, wd)
    cross = [lax.ppermute(w, "dp", SWAP) for w in theirs]
    arrived = lax.all_to_all(
        send.reshape(E, PAIR, DW), "expert", 0, 0, tiled=True
    ).reshape(SEND, DW)
    rows = call(sort_kernel, pair16, 1, scratch_shapes=sort)(arrived)
    other = lax.ppermute(rows, "dp", SWAP)
    home, *held = call(
        home_kernel,
        (wide32, *half[:2]),
        3,
        in_specs=[VMEM, VMEM, hbm],
        scratch_shapes=[pltpu.SemaphoreType.DMA((2,))],
        **work,
    )(rows, held_down, wgu)
    held.append(held_down)
    chip = call(join_kernel, wide16, 5, **work)(home, other, *cross)
    got = lax.all_to_all(
        chip.reshape(RING, RX, 3 * H), "dp", 0, 0, axis_index_groups=FIRST, tiled=True
    )
    chunk = call(sum_kernel, chunk16, 1)(got)
    parts = lax.all_gather(chunk, "dp", axis=0, axis_index_groups=SECOND, tiled=True)
    act = call(act_kernel, chunk16, 1)(parts)
    mine = lax.all_gather(act, "dp", axis=0, axis_index_groups=FIRST, tiled=True)
    mine = mine.reshape(ROWS, 3 * H)
    terms = call(other_kernel, pair16, 4, **work)(mine, *cross)
    got = lax.ppermute(terms, "dp", SWAP)
    pick = sds(((TOPK + 1) * TOK, SEND), BF16)
    terms, pick = call(first_kernel, (pair32, pick), 5, **work)(mine, *held, place)
    sort[1] = pltpu.VMEM((SEND, DW), F32)
    back = call(finish_kernel, pair16, 2, scratch_shapes=sort)(terms, got)
    returned = lax.all_to_all(
        back.reshape(E, PAIR, DW), "expert", 0, 0, tiled=True
    ).reshape(SEND, DW)
    shape = sds((TOK, DW), BF16)
    return call(combine_kernel, (shape, shape), 3)(returned, weight, pick)


def solution(mesh):
    rows, cols = P("expert", "dp"), P("expert", None)
    return jax.shard_map(
        local,
        mesh=mesh,
        in_specs=(rows, P("expert", "dp", None), P("expert", None, "dp"), cols, cols, rows),
        out_specs=(rows, rows),
        check_vma=False,
    )
```
